128 devices in a mesh: patch: 64 (over x, y_hi, z, core), head: 2 (over y_lo).
Axes of the slice: x: 4, y: 4 (y_hi: 2, y_lo: 2; y = y_hi * 2 + y_lo), z: 4, core: 2. Of those that a mesh axis runs over, the one named last changes fastest.
Arguments:
- image: bfloat16 [8192, 3072], P(('patch', 'head')), may hold values from -6 to 6
- w_qkv: bfloat16 [3072, 3, 1792], P(None, None, 'head'), may hold values from -0.109375 to 0.109375
- qk_gain: float32 [2, 128], replicated, may hold values from 0.1 to 1.9
- stale_kv: bfloat16 [2, 8192, 1792], P(None, 'patch', 'head')
- text_kv: bfloat16 [2, 512, 1792], P(None, None, 'head'), may hold values from -6 to 6
- text_count: int32 [1], replicated, may hold values from 128 to 512
- row_offset: int32 [64], P('patch'), may hold values from 0 to 63, as said below
- w_out: bfloat16 [1792, 3072], P('head'), may hold values from -0.125 to 0.125
Outputs:
- mixed: bfloat16 [8192, 3072], P(('patch', 'head'))
- fresh_kv: bfloat16 [2, 8192, 1792], P(None, 'patch', 'head')
The draws below stay inside these ranges and needn't reach their ends.
Inputs may be any that keep to these rules, and one draw needn't show every extreme that they name: `row_offset`: A permutation of 0, 1, 2, ...: each patch starts at a different multiple of 1.
All inputs are finite; a program needn't handle non-finite values.
Results may differ from the reference program's by a relative error of at most 0.015.
Values may be sent and summed in bfloat16 or wider, within the bound.
No kernel may reach another device: no remote copies, remote signals or barrier semaphores. Data moves between devices by JAX's collectives and lax.ppermute only.
A program may use at most 192 MiB of HBM per device.

```python
import jax
import jax.numpy as jnp
from jax import lax

D = 3072
HEADS = 14
HD = 128
COLS = 128
ROWS_DEV = 1
TEXT = 512
TOK = 128
IMG = 8192
N_PATCH = 64


def draw_stale_kv(key, part):
    key = jax.random.fold_in(key, 11)
    third_key = jax.random.fold_in(key, 2)
    base = jax.random.normal(third_key, (2, IMG, HEADS * HD), jnp.float32)
    return base.astype(jnp.bfloat16)


def draw_row_offset(key, part):
    key = jax.random.fold_in(key, 5)
    return (jax.random.permutation(key, N_PATCH) * ROWS_DEV).astype(jnp.int32)


def block_levels(key, shape, cuts, smallest, largest):
    level = 1.0
    for dim, blocks in cuts:
        heights = jax.random.uniform(jax.random.fold_in(jax.random.fold_in(key, 6), dim), (blocks,), jnp.float32, smallest / len(cuts), largest / len(cuts))
        level = level * jnp.repeat(jnp.exp(heights), shape[dim] // blocks).reshape((-1,) + (1,) * (len(shape) - 1 - dim))
    return level


def scatter_about(rng, shape, width, reach, cuts=(), kind=jnp.bfloat16):
    values = jax.random.normal(rng, shape, jnp.float32) * width
    if len(cuts) > 0:
        values = block_levels(rng, shape, cuts, -0.22, 0.18) * values
    return jnp.clip(values, min=-reach, max=reach).astype(kind)


def setup_inputs(seed: int = 0) -> dict:
    arg_keys = jax.random.split(jax.random.key(seed), 9)
    return {
        "image": scatter_about(arg_keys[0], (IMG, D), 1.0, 6.0, ((0, 128),)),
        "w_qkv": scatter_about(arg_keys[1], (D, 3, HEADS * HD), D ** -0.5, 0.109375, ((2, 2),)),
        "qk_gain": jnp.clip(1.0 + 0.18 * jax.random.normal(arg_keys[2], (2, HD), jnp.float32), 0.1, 1.9),
        "stale_kv": draw_stale_kv(jax.random.fold_in(arg_keys[8], 71), 0),
        "text_kv": scatter_about(arg_keys[4], (2, TEXT, HEADS * HD), 1.0, 6.0, ((2, 2),)),
        "text_count": jax.random.randint(arg_keys[5], (1,), TEXT // 4, TEXT + 1).astype(jnp.int32),
        "row_offset": draw_row_offset(jax.random.fold_in(arg_keys[8], 71), 0),
        "w_out": scatter_about(arg_keys[7], (HEADS * HD, D), (HEADS * HD) ** -0.5, 0.125, ((0, 2),)),
    }


def rope_angles(rows, cols):
    first = HD // 8
    band = (HD - first) // 2
    omega = 10000.0 ** (-2.0 * jnp.arange(band // 2, dtype=jnp.float32) / band)
    zeros = jnp.zeros((rows.shape[0], first // 2), jnp.float32)
    return jnp.concatenate([zeros, rows[:, None] * omega[None, :], cols[:, None] * omega[None, :]], axis=1)

def rotate(vectors, angles):
    count, heads = (vectors.shape[0], vectors.shape[1])
    pairs = vectors.reshape(count, heads, HD // 2, 2)
    cosine = jnp.cos(angles)[:, None, :]
    sine = jnp.sin(angles)[:, None, :]
    first = pairs[..., 0]
    second = pairs[..., 1]
    turned = jnp.stack([first * cosine - second * sine, first * sine + second * cosine], axis=-1)
    return turned.reshape(count, heads, HD)

def normalize(vectors, gain):
    return vectors * lax.rsqrt(lax.optimization_barrier(jnp.mean(vectors * vectors, axis=-1, keepdims=True)) + 1e-06) * gain

def reference(image, w_qkv, qk_gain, stale_kv, text_kv, text_count, row_offset, w_out):
    projected = jnp.dot(image, w_qkv.reshape(D, 3 * HEADS * HD), preferred_element_type=jnp.float32)
    projected = projected.reshape(IMG, 3, HEADS, HD)
    token_ids = jnp.arange(IMG, dtype=jnp.int32)
    patch_ids = token_ids // TOK
    within = token_ids % TOK
    rows = (row_offset[patch_ids] + within // COLS).astype(jnp.float32)
    cols = (within % COLS).astype(jnp.float32)
    angles = rope_angles(rows, cols)
    queries = rotate(normalize(projected[:, 0], qk_gain[0]), angles).astype(jnp.bfloat16)
    keys_new = rotate(normalize(projected[:, 1], qk_gain[1]), angles).astype(jnp.bfloat16)
    values_new = projected[:, 2].astype(jnp.bfloat16)
    fresh_kv = jnp.stack([keys_new.reshape(IMG, HEADS * HD), values_new.reshape(IMG, HEADS * HD)])
    stale_keys = stale_kv[0].reshape(IMG, HEADS, HD)
    stale_values = stale_kv[1].reshape(IMG, HEADS, HD)
    text_keys = text_kv[0].reshape(TEXT, HEADS, HD)
    text_values = text_kv[1].reshape(TEXT, HEADS, HD)
    valid = jnp.concatenate([jnp.arange(TEXT, dtype=jnp.int32) < text_count[0], jnp.ones((IMG,), bool)])
    scale = 1.0 / jnp.sqrt(jnp.float32(HD))

    def one_patch(patch):
        mine = (patch_ids == patch)[:, None, None]
        all_keys = jnp.concatenate([text_keys, jnp.where(mine, keys_new, stale_keys)], axis=0)
        all_values = jnp.concatenate([text_values, jnp.where(mine, values_new, stale_values)], axis=0)
        start = (patch * TOK).astype(jnp.int32)
        local_q = lax.dynamic_slice_in_dim(queries, start, TOK, 0)
        scores = jnp.einsum('qhd,khd->hqk', local_q.astype(jnp.float32), all_keys.astype(jnp.float32)) * scale
        scores = jnp.where(valid[None, None, :], scores, -jnp.inf)
        peak = lax.optimization_barrier(jnp.max(scores, axis=-1, keepdims=True))
        raw = jnp.where(valid[None, None, :], jnp.exp(scores - peak), 0.0)
        total = lax.optimization_barrier(jnp.sum(raw, axis=-1, keepdims=True))
        raw_bf = raw.astype(jnp.bfloat16)
        mixed_heads = jnp.einsum('hqk,khd->hqd', raw_bf.astype(jnp.float32), all_values.astype(jnp.float32)) / total
        return jnp.transpose(mixed_heads, (1, 0, 2)).reshape(TOK, HEADS * HD).astype(jnp.bfloat16)
    attended = lax.map(one_patch, jnp.arange(N_PATCH, dtype=jnp.int32)).reshape(IMG, HEADS * HD)
    mixed = jnp.dot(attended, w_out, preferred_element_type=jnp.float32).astype(jnp.bfloat16)
    return (mixed, fresh_kv)
```

```python
import functools
import math

import jax
import jax.numpy as jnp
import numpy as np
from jax import lax
from jax.experimental import pallas as pl
from jax.experimental.pallas import tpu as pltpu
from jax.sharding import PartitionSpec as P

D = 3072
HD = 128
COLS = 128
HEADS = 7
MINE = 3
UNITS = 7
TOK = 128
FEAT = HEADS * HD
STEP = 512
SCALE2 = math.log2(math.e) / math.sqrt(HD)
F32 = jnp.float32
BF16 = jnp.bfloat16
VMEM_LIMIT = 48 * 1024 * 1024


def _place(x, y, z, c):
    return ((x * 2 + y) * 4 + z) * 2 + c


def _perm(move):
    pairs = []
    for p in range(64):
        x, y, z, c = p // 16, (p // 8) % 2, (p // 2) % 4, p % 2
        pairs.append((p, _place(*move(x, y, z, c))))
    return pairs


def _key_move(d):
    return lambda x, y, z, c: ((x + d) % 4, y, z, c) if c == 0 else (x, y, (z + d) % 4, c)


def _query_move(d):
    return lambda x, y, z, c: (x, y, (z + d) % 4, c) if c == 0 else ((x + d) % 4, y, z, c)


def _core_move(x, y, z, c):
    return (x, y, z, 1 - c)


def _y_move(x, y, z, c):
    return (x, 1 - y, z, c)


def move(array, how):
    return lax.ppermute(array, "patch", _perm(how))


def swap_heads(array):
    return lax.ppermute(array, "head", [(0, 1), (1, 0)])


def _turn(v, gain, cosine, sine):
    v = v * lax.rsqrt(jnp.mean(v * v, axis=-1, keepdims=True) + 1e-06) * gain
    lane = lax.broadcasted_iota(jnp.int32, v.shape, 1)
    other = jnp.where(lane % 2 == 0, pltpu.roll(v, HD - 1, 1), pltpu.roll(v, 1, 1))
    return (v * cosine + other * sine).astype(BF16)


def _tokens(place, own_ref, oth_ref, x_ref):
    h = place[1]
    half = own_ref.shape[0]
    x_ref[pl.ds(pl.multiple_of(h * half, half), half), :] = own_ref[...]
    x_ref[pl.ds(pl.multiple_of((1 - h) * half, half), half), :] = oth_ref[...]


def _query_kernel(place, own_ref, oth_ref, w_ref, gain_ref, cos_ref, sin_ref, qa_ref, qb_ref, x_ref, acc_ref):
    k = pl.program_id(0)
    _tokens(place, own_ref, oth_ref, x_ref)

    @pl.when(k == 0)
    def _():
        acc_ref[...] = jnp.zeros_like(acc_ref)

    acc_ref[...] += jnp.dot(x_ref[...], w_ref[0], preferred_element_type=F32)

    @pl.when(k == pl.num_programs(0) - 1)
    def _():
        for head in range(HEADS):
            q = _turn(acc_ref[:, head * HD : (head + 1) * HD], gain_ref[0:1, :], cos_ref[...], sin_ref[...])
            if head == MINE:
                qa_ref[MINE] = q
                continue
            low = head < MINE

            @pl.when(place[0] == (0 if low else 1))
            def _():
                qa_ref[head if low else head - MINE - 1] = q

            @pl.when(place[0] == (1 if low else 0))
            def _():
                qb_ref[head if low else head - MINE - 1] = q


def _kv_kernel(place, own_ref, oth_ref, w_ref, gain_ref, cos_ref, sin_ref, out_ref, x_ref, acc_ref):
    j = pl.program_id(0)
    k = pl.program_id(1)
    _tokens(place, own_ref, oth_ref, x_ref)

    @pl.when(k == 0)
    def _():
        acc_ref[...] = jnp.zeros_like(acc_ref)

    acc_ref[...] += jnp.dot(x_ref[...], w_ref[0], preferred_element_type=F32)

    @pl.when(k == pl.num_programs(1) - 1)
    def _():
        @pl.when(j == 0)
        def _():
            for head in range(HEADS):
                at = slice(head * HD, (head + 1) * HD)
                out_ref[0, :, at] = _turn(acc_ref[:, at], gain_ref[1:2, :], cos_ref[...], sin_ref[...])

        @pl.when(j == 1)
        def _():
            out_ref[0] = acc_ref[...].astype(BF16)


def project_queries(place, own, oth, w, gain, cosine, sine):
    half = own.shape[0]
    steps = D // STEP
    return pl.pallas_call(
        _query_kernel,
        grid_spec=pltpu.PrefetchScalarGridSpec(
            num_scalar_prefetch=1,
            grid=(steps,),
            in_specs=[
                pl.BlockSpec((half, STEP), lambda k, s: (0, k)),
                pl.BlockSpec((half, STEP), lambda k, s: (0, k)),
                pl.BlockSpec((1, STEP, FEAT), lambda k, s: (0, k, 0)),
                pl.BlockSpec((2, HD), lambda k, s: (0, 0)),
                pl.BlockSpec((TOK, HD), lambda k, s: (0, 0)),
                pl.BlockSpec((TOK, HD), lambda k, s: (0, 0)),
            ],
            out_specs=[
                pl.BlockSpec((MINE + 1, TOK, HD), lambda k, s: (0, 0, 0)),
                pl.BlockSpec((MINE, TOK, HD), lambda k, s: (0, 0, 0)),
            ],
            scratch_shapes=[pltpu.VMEM((TOK, STEP), BF16), pltpu.VMEM((TOK, FEAT), F32)],
        ),
        out_shape=[
            jax.ShapeDtypeStruct((MINE + 1, TOK, HD), BF16),
            jax.ShapeDtypeStruct((MINE, TOK, HD), BF16),
        ],
        compiler_params=pltpu.CompilerParams(vmem_limit_bytes=VMEM_LIMIT),
        name="query_projection",
    )(place, own, oth, w, gain, cosine, sine)


def project_keys(place, own, oth, w, gain, cosine, sine):
    half = own.shape[0]
    steps = D // STEP
    return pl.pallas_call(
        _kv_kernel,
        grid_spec=pltpu.PrefetchScalarGridSpec(
            num_scalar_prefetch=1,
            grid=(2, steps),
            in_specs=[
                pl.BlockSpec((half, STEP), lambda j, k, s: (0, k)),
                pl.BlockSpec((half, STEP), lambda j, k, s: (0, k)),
                pl.BlockSpec((1, STEP, FEAT), lambda j, k, s: (j + 1, k, 0)),
                pl.BlockSpec((2, HD), lambda j, k, s: (0, 0)),
                pl.BlockSpec((TOK, HD), lambda j, k, s: (0, 0)),
                pl.BlockSpec((TOK, HD), lambda j, k, s: (0, 0)),
            ],
            out_specs=pl.BlockSpec((1, TOK, FEAT), lambda j, k, s: (j, 0, 0)),
            scratch_shapes=[pltpu.VMEM((TOK, STEP), BF16), pltpu.VMEM((TOK, FEAT), F32)],
        ),
        out_shape=jax.ShapeDtypeStruct((2, TOK, FEAT), BF16),
        compiler_params=pltpu.CompilerParams(vmem_limit_bytes=VMEM_LIMIT),
        name="key_value_projection",
    )(place, own, oth, w, gain, cosine, sine)


def _head_of(u, c):
    low = jnp.where(u > MINE, u - MINE - 1, u)
    return jnp.where(u == MINE, MINE, low + (MINE + 1) * c)


def _slot_of(u, c):
    low = jnp.where(u > MINE, u - MINE - 1, u)
    return jnp.where(u == MINE, MINE * (1 - c), low + c)


def _scores(q, k):
    return lax.dot_general(q, k, (((1,), (1,)), ((), ())), preferred_element_type=F32)


def _fold(state, scores, values):
    peak = jnp.max(scores[0], axis=1, keepdims=True)
    for s in scores[1:]:
        peak = jnp.maximum(peak, jnp.max(s, axis=1, keepdims=True))
    if state is not None:
        peak = jnp.maximum(peak, state[0])
    total = None
    out = None
    for s, v in zip(scores, values, strict=True):
        raw = jnp.exp2((s - peak) * SCALE2)
        part = jnp.sum(raw, axis=1, keepdims=True)
        total = part if total is None else total + part
        upd = jnp.dot(raw.astype(BF16), v, preferred_element_type=F32)
        out = upd if out is None else out + upd
    if state is not None:
        factor = jnp.exp2((state[0] - peak) * SCALE2)
        total = total + state[1] * factor
        out = out + state[2] * factor
    return peak, total, out


def _pack(peak, total):
    lane = lax.broadcasted_iota(jnp.int32, (peak.shape[0], HD), 1)
    return jnp.where(lane < HD // 2, peak, total)


def _home_kernel(place, count, q_ref, text_ref, fresh_ref, sib_ref, pair_ref, acc_ref, stat_ref):
    u = pl.program_id(0)
    q = q_ref[0]
    own = u <= MINE
    text = _scores(q, text_ref[0])
    slot = lax.broadcasted_iota(jnp.int32, text.shape, 1)
    text = jnp.where(slot < count[0], text, -jnp.inf)
    fresh = jnp.where(own, fresh_ref[...], sib_ref[...])
    stale = jnp.where(own, pair_ref[:, TOK:], pair_ref[:, :TOK])
    peak, total, out = _fold(
        None,
        [text, _scores(q, fresh[0]), _scores(q, stale[0])],
        [text_ref[1], fresh[1], stale[1]],
    )
    acc_ref[0] = out
    stat_ref[0] = _pack(peak, total)


def attend_home(place, count, queries, text_kv, fresh, sibling, pair):
    text_slots = text_kv.shape[1]
    return pl.pallas_call(
        _home_kernel,
        grid_spec=pltpu.PrefetchScalarGridSpec(
            num_scalar_prefetch=2,
            grid=(UNITS,),
            in_specs=[
                pl.BlockSpec((1, TOK, HD), lambda u, s, n: (u, 0, 0)),
                pl.BlockSpec((2, text_slots, HD), lambda u, s, n: (0, 0, _head_of(u, s[0]))),
                pl.BlockSpec((2, TOK, HD), lambda u, s, n: (0, 0, _head_of(u, s[0]))),
                pl.BlockSpec((2, TOK, HD), lambda u, s, n: (0, 0, jnp.maximum(u - MINE - 1, 0))),
                pl.BlockSpec((2, 2 * TOK, HD), lambda u, s, n: (0, 0, _slot_of(u, s[0]))),
            ],
            out_specs=[
                pl.BlockSpec((1, TOK, HD), lambda u, s, n: (u, 0, 0)),
                pl.BlockSpec((1, TOK, HD), lambda u, s, n: (u, 0, 0)),
            ],
        ),
        out_shape=[jax.ShapeDtypeStruct((UNITS, TOK, HD), F32)] * 2,
        compiler_params=pltpu.CompilerParams(vmem_limit_bytes=VMEM_LIMIT),
        name="home_attention",
    )(place, count, queries, text_kv, fresh, sibling, pair)


def _near_kernel(place, q0, q1, q2, q3, acc_in, stat_in, k0, k1, k2, k3, acc_ref, stat_ref, q_ref):
    q_ref[0:TOK] = q0[0]
    q_ref[TOK : 2 * TOK] = q1[0]
    q_ref[2 * TOK : 3 * TOK] = q2[0]
    q_ref[3 * TOK :] = q3[0]
    far = [k1, k2, k3]
    state = (stat_in[0, :, 0:1], stat_in[0, :, HD // 2 : HD // 2 + 1], acc_in[0])
    q = q_ref[0:TOK]
    peak, total, out = _fold(state, [_scores(q, k[0]) for k in far], [k[1] for k in far])
    acc_ref[0, 0:TOK] = out
    stat_ref[0, 0:TOK] = _pack(peak, total)
    q = q_ref[TOK:]
    blocks = [k0] + far
    peak, total, out = _fold(None, [_scores(q, k[0]) for k in blocks], [k[1] for k in blocks])
    acc_ref[0, TOK:] = out
    stat_ref[0, TOK:] = _pack(peak, total)


def _pair_spec():
    return pl.BlockSpec((2, 2 * TOK, HD), lambda u, s: (0, 0, _slot_of(u, s[0])))


def _unit_spec(rows=TOK):
    return pl.BlockSpec((1, rows, HD), lambda u, s: (u, 0, 0))


def attend_near(place, queries, acc, stat, pairs):
    rows = 4 * TOK
    return pl.pallas_call(
        _near_kernel,
        grid_spec=pltpu.PrefetchScalarGridSpec(
            num_scalar_prefetch=1,
            grid=(UNITS,),
            in_specs=[_unit_spec()] * 6 + [_pair_spec()] * 4,
            out_specs=[_unit_spec(rows)] * 2,
            scratch_shapes=[pltpu.VMEM((rows, HD), BF16)],
        ),
        out_shape=[jax.ShapeDtypeStruct((UNITS, rows, HD), F32)] * 2,
        compiler_params=pltpu.CompilerParams(vmem_limit_bytes=VMEM_LIMIT),
        name="near_attention",
    )(place, *queries, acc, stat, *pairs)


def _far_kernel(place, q0, q1, q2, q3, acc_in, stat_in, k0, k1, k2, k3, o0, o1, o2, o3, q_ref):
    u = pl.program_id(0)
    q_ref[0:TOK] = q0[0]
    q_ref[TOK : 2 * TOK] = q1[0]
    q_ref[2 * TOK : 3 * TOK] = q2[0]
    q_ref[3 * TOK :] = q3[0]
    blocks = [k0, k1, k2, k3]
    state = (stat_in[0, :, 0:1], stat_in[0, :, HD // 2 : HD // 2 + 1], acc_in[0])
    q = q_ref[...]
    peak, total, out = _fold(state, [_scores(q, k[0]) for k in blocks], [k[1] for k in blocks])
    out = (out / total).astype(BF16)
    level = peak * SCALE2 + jnp.log2(total)
    high = level.astype(BF16).astype(F32)
    middle = (level - high).astype(BF16).astype(F32)
    low = level - high - middle
    lane = lax.broadcasted_iota(jnp.int32, (4 * TOK, HD), 1)
    mark = jnp.where(
        lane == u, high, jnp.where(lane == u + 16, middle, jnp.where(lane == u + 32, low, 0.0))
    ).astype(BF16)
    for i, o in enumerate((o0, o1, o2, o3)):
        at = slice(i * TOK, (i + 1) * TOK)
        o[u] = out[at]

        @pl.when(u == 0)
        def _():
            o[UNITS] = mark[at]

        @pl.when(u > 0)
        def _():
            o[UNITS] += mark[at]


def attend_far(place, queries, acc, stat, pairs):
    rows = 4 * TOK
    return pl.pallas_call(
        _far_kernel,
        grid_spec=pltpu.PrefetchScalarGridSpec(
            num_scalar_prefetch=1,
            grid=(UNITS,),
            in_specs=[_unit_spec()] * 4 + [_unit_spec(rows)] * 2 + [_pair_spec()] * 4,
            out_specs=[pl.BlockSpec((UNITS + 1, TOK, HD), lambda u, s: (0, 0, 0))] * 4,
            scratch_shapes=[pltpu.VMEM((rows, HD), BF16)],
        ),
        out_shape=[jax.ShapeDtypeStruct((UNITS + 1, TOK, HD), BF16)] * 4,
        compiler_params=pltpu.CompilerParams(vmem_limit_bytes=VMEM_LIMIT),
        name="far_attention",
    )(place, *queries, acc, stat, *pairs)


def _merge_kernel(p0, p1, p2, p3, mine_ref, sib_ref):
    parts = (p0, p1, p2, p3)
    levels = []
    for p in parts:
        mark = p[UNITS].astype(F32)
        levels.append(mark + pltpu.roll(mark, HD - 16, 1) + pltpu.roll(mark, HD - 32, 1))
    top = jnp.maximum(jnp.maximum(levels[0], levels[1]), jnp.maximum(levels[2], levels[3]))
    weights = [jnp.exp2(v - top) for v in levels]
    total = weights[0] + weights[1] + weights[2] + weights[3]
    weights = [w / total for w in weights]
    for u in range(UNITS):
        out = None
        for p, w in zip(parts, weights, strict=True):
            term = p[u].astype(F32) * w[:, u : u + 1]
            out = term if out is None else out + term
        if u <= MINE:
            mine_ref[u] = out.astype(BF16)
        else:
            sib_ref[u - MINE - 1] = out.astype(BF16)


def merge(parts):
    return pl.pallas_call(
        _merge_kernel,
        out_shape=[
            jax.ShapeDtypeStruct((MINE + 1, TOK, HD), BF16),
            jax.ShapeDtypeStruct((MINE, TOK, HD), BF16),
        ],
        compiler_params=pltpu.CompilerParams(vmem_limit_bytes=VMEM_LIMIT),
        name="merge_parts",
    )(*parts)


def _out_kernel(place, mine_ref, got_ref, w_ref, keep_ref, send_ref, a_ref):
    half = keep_ref.shape[0]

    @pl.when(pl.program_id(0) == 0)
    def _():
        a_ref[:, MINE * HD : (MINE + 1) * HD] = mine_ref[MINE]
        for i in range(MINE):
            low = slice(i * HD, (i + 1) * HD)
            high = slice((MINE + 1 + i) * HD, (MINE + 2 + i) * HD)

            @pl.when(place[0] == 0)
            def _():
                a_ref[:, low] = mine_ref[i]
                a_ref[:, high] = got_ref[i]

            @pl.when(place[0] == 1)
            def _():
                a_ref[:, low] = got_ref[i]
                a_ref[:, high] = mine_ref[i]

    out = jnp.dot(a_ref[...], w_ref[...], preferred_element_type=F32)

    @pl.when(place[1] == 0)
    def _():
        keep_ref[...] = out[:half]
        send_ref[...] = out[half:].astype(BF16)

    @pl.when(place[1] == 1)
    def _():
        keep_ref[...] = out[half:]
        send_ref[...] = out[:half].astype(BF16)


def project_out(place, mine, got, w_out):
    half = TOK // 2
    cut = 768
    return pl.pallas_call(
        _out_kernel,
        grid_spec=pltpu.PrefetchScalarGridSpec(
            num_scalar_prefetch=1,
            grid=(D // cut,),
            in_specs=[
                pl.BlockSpec((MINE + 1, TOK, HD), lambda n, s: (0, 0, 0)),
                pl.BlockSpec((MINE, TOK, HD), lambda n, s: (0, 0, 0)),
                pl.BlockSpec((FEAT, cut), lambda n, s: (0, n)),
            ],
            out_specs=[
                pl.BlockSpec((half, cut), lambda n, s: (0, n)),
                pl.BlockSpec((half, cut), lambda n, s: (0, n)),
            ],
            scratch_shapes=[pltpu.VMEM((TOK, FEAT), BF16)],
        ),
        out_shape=[
            jax.ShapeDtypeStruct((half, D), F32),
            jax.ShapeDtypeStruct((half, D), BF16),
        ],
        compiler_params=pltpu.CompilerParams(vmem_limit_bytes=VMEM_LIMIT),
        name="output_projection",
    )(place, mine, got, w_out)


def _bands():
    first = HD // 8
    band = (HD - first) // 2
    omega = np.repeat(10000.0 ** (-2.0 * np.arange(band // 2) / band), 2)
    along_rows = np.zeros((HD,))
    along_cols = np.zeros((HD,))
    along_rows[first : first + band] = omega
    along_cols[first + band :] = omega
    sign = np.where(np.arange(HD) % 2 == 0, -1.0, 1.0)
    return (v.astype(np.float32)[None, :] for v in (along_rows, along_cols, sign))


def body(image, w_qkv, qk_gain, stale_kv, text_kv, text_count, row_offset, w_out):
    core = lax.axis_index("patch") % 2
    place = jnp.stack([core, lax.axis_index("head")]).astype(jnp.int32)
    other_image = swap_heads(image)

    wide = (2, TOK, (MINE + 1) * HD)
    given = lax.dynamic_slice(stale_kv, (0, 0, (1 - core) * MINE * HD), wide)
    kept = lax.dynamic_slice(stale_kv, (0, 0, core * MINE * HD), wide)
    pair = jnp.concatenate([kept, move(given, _core_move)], axis=1)
    far_pair = move(pair, _y_move)
    near = [pair] + [move(pair, _key_move(d)) for d in (1, 3, 2)]
    far = [far_pair] + [move(far_pair, _key_move(d)) for d in (1, 3, 2)]

    within = jnp.arange(TOK, dtype=jnp.int32)
    rows = (row_offset[0] + within // COLS).astype(F32)[:, None]
    cols = (within % COLS).astype(F32)[:, None]
    along_rows, along_cols, sign = _bands()
    angles = rows * along_rows + cols * along_cols
    cosine = jnp.cos(angles)
    sine = jnp.sin(angles) * sign

    w = jnp.transpose(w_qkv, (1, 0, 2))
    q_mine, q_given = project_queries(place, image, other_image, w, qk_gain, cosine, sine)
    units = jnp.concatenate([q_mine, move(q_given, _core_move)], axis=0)
    queries = [units] + [move(units, _query_move(d)) for d in (1, 3, 2)]
    fresh_kv = project_keys(place, image, other_image, w, qk_gain, cosine, sine)
    fresh_given = lax.dynamic_slice(
        fresh_kv, (0, 0, (1 - core) * (MINE + 1) * HD), (2, TOK, MINE * HD)
    )
    sibling = move(fresh_given, _core_move)

    acc, stat = attend_home(place, text_count, units, text_kv, fresh_kv, sibling, pair)
    acc, stat = attend_near(place, queries, acc, stat, near)
    parts = attend_far(place, queries, acc, stat, far)
    back = [parts[0]] + [move(parts[i], _query_move(d)) for i, d in ((1, 3), (2, 1), (3, 2))]
    mine, given_back = merge(back)
    keep, send = project_out(place, mine, move(given_back, _core_move), w_out)
    mixed = (keep + swap_heads(send).astype(F32)).astype(BF16)
    return (mixed, fresh_kv)


def solution(mesh):
    placed = (
        P(("patch", "head"), None),
        P(None, None, "head"),
        P(),
        P(None, "patch", "head"),
        P(None, None, "head"),
        P(),
        P("patch"),
        P("head", None),
    )
    return jax.shard_map(
        body,
        mesh=mesh,
        in_specs=placed,
        out_specs=(P(("patch", "head"), None), P(None, "patch", "head")),
        check_vma=False,
    )
```

```python
import functools
import math

import jax
import jax.numpy as jnp
import numpy as np
from jax import lax
from jax.experimental import pallas as pl
from jax.experimental.pallas import tpu as pltpu
from jax.sharding import PartitionSpec as P

D = 3072
HD = 128
COLS = 128
HEADS = 7
MINE = 3
UNITS = 7
TOK = 128
FEAT = HEADS * HD
HALF = TOK // 2
PIECES = 6
STEP = D // PIECES
SCALE2 = math.log2(math.e) / math.sqrt(HD)
F32 = jnp.float32
HBM = "hbm"
BF16 = jnp.bfloat16
MIB = 1024 * 1024
COST = pl.CostEstimate(flops=1, transcendentals=0, bytes_accessed=1)
SMEM = pl.BlockSpec(memory_space=pltpu.SMEM)
VMEM = pl.BlockSpec(memory_space=pltpu.VMEM)
ANY = pl.BlockSpec(memory_space=pl.ANY)


def _place(x, y, z, c):
    return ((x * 2 + y) * 4 + z) * 2 + c


def _perm(move):
    pairs = []
    for p in range(64):
        x, y, z, c = p // 16, (p // 8) % 2, (p // 2) % 4, p % 2
        pairs.append((p, _place(*move(x, y, z, c))))
    return pairs


def _key_move(d):
    return lambda x, y, z, c: ((x + d) % 4, y, z, c) if c == 0 else (x, y, (z + d) % 4, c)


def _query_move(d):
    return lambda x, y, z, c: (x, y, (z + d) % 4, c) if c == 0 else ((x + d) % 4, y, z, c)


def _core_move(x, y, z, c):
    return (x, y, z, 1 - c)


def _y_move(x, y, z, c):
    return (x, 1 - y, z, c)


def move(array, how):
    return lax.ppermute(array, "patch", _perm(how))


def swap_heads(array):
    return lax.ppermute(array, "head", [(0, 1), (1, 0)])


def kernel_call(kernel, name, out_shape, scratch_shapes, scalars, *arrays, after=(), outside=(), limit=12):
    first, count = len(scalars) + len(outside) + len(arrays), len(after)

    def run(*refs):
        kernel(*refs[:first], *refs[first + count :])

    return pl.pallas_call(
        run,
        in_specs=[SMEM] * len(scalars) + [ANY] * len(outside) + [VMEM] * len(arrays) + [ANY] * count,
        out_specs=[VMEM] * len(out_shape),
        out_shape=[pltpu.VMEM(*s) if len(s) == 2 else jax.ShapeDtypeStruct(*s[:2]) for s in out_shape],
        scratch_shapes=[pltpu.VMEM(*s) if isinstance(s, tuple) else s for s in scratch_shapes],
        compiler_params=pltpu.CompilerParams(vmem_limit_bytes=limit * MIB),
        cost_estimate=COST,
        name=name,
    )(*scalars, *(pltpu.with_memory_space_constraint(a, pltpu.HBM) for a in outside), *arrays, *after)


def _turn(v, table_ref, which):
    v = v * lax.rsqrt(jnp.mean(v * v, axis=-1, keepdims=True) + 1e-06)
    lane = lax.broadcasted_iota(jnp.int32, v.shape, 1)
    other = jnp.where(lane % 2 == 0, pltpu.roll(v, HD - 1, 1), pltpu.roll(v, 1, 1))
    return v * table_ref[2 * which] + other * table_ref[2 * which + 1]


def _bring(w_ref, which, out_ref, sems):
    groups = []
    for j, i in enumerate(which):
        copies = []
        for k in range(PIECES):
            rows = pl.ds(k * STEP, STEP)
            copies.append(pltpu.make_async_copy(w_ref.at[i, rows], out_ref.at[j, rows], sems.at[j * PIECES + k]))
        for copy in copies:
            copy.start()
        groups.append(copies)
    return groups


def _stage_kernel(w_ref, out_ref, sems):
    for copy in _bring(w_ref, (0,), out_ref, sems)[0]:
        copy.wait()


def stage(w, after):
    scratch = [pltpu.SemaphoreType.DMA((PIECES,))]
    outs = [((1, D, FEAT), BF16)]
    return kernel_call(_stage_kernel, "stage_weights", outs, scratch, [], outside=[w], after=after)[0]


def _query_kernel(place, w_ref, oth_ref, own_ref, table_ref, qa_ref, qb_ref, q_ref, x_ref):
    x = jnp.concatenate([oth_ref[...], own_ref[...]], axis=0)
    x_ref[...] = x
    projected = jnp.dot(x, w_ref[0], preferred_element_type=F32)
    queries = []
    for head in range(HEADS):
        at = slice(head * HD, (head + 1) * HD)
        queries.append((_turn(projected[:, at], table_ref, 0) * SCALE2).astype(BF16))
        q_ref[head] = queries[head]
    qa_ref[MINE] = queries[MINE]
    first = place[0] == 0
    for i in range(MINE):
        low, high = queries[i], queries[i + MINE + 1]
        qa_ref[i] = jnp.where(first, low, high)
        qb_ref[i] = jnp.where(first, high, low)


def project_queries(place, *arrays):
    outs = [
        ((MINE + 1, TOK, HD), BF16),
        ((MINE, TOK, HD), BF16),
        ((HEADS, TOK, HD), BF16),
        ((TOK, D), BF16),
    ]
    return kernel_call(_query_kernel, "query_projection", outs, [], [place], *arrays)


def _home_kernel(
    place, count, w_ref, text_ref, x_ref, table_ref, q_ref, out_ref, home_ref, stat_ref, buffer, text, part, sems
):
    bring_text = pltpu.make_async_copy(text_ref, text, sems.at[2 * PIECES])
    bring_text.start()
    groups = _bring(w_ref, (1, 2), buffer, sems)
    first = pl.ds(pl.multiple_of((1 - place[1]) * HALF, HALF), HALF)
    second = pl.ds(pl.multiple_of(place[1] * HALF, HALF), HALF)
    bring_text.wait()
    peaks = []
    for head in range(HEADS):
        at = slice(head * HD, (head + 1) * HD)
        s = _scores(q_ref[head], text[0, :, at])
        s = jnp.where(_lane(s.shape) < count[0], s, -jnp.inf)
        peak, part[head] = _fold(s, None, text[1, :, at])
        peaks.append(peak)
    for copy in groups[0]:
        copy.wait()
    projected = jnp.dot(x_ref[...], buffer[0], preferred_element_type=F32)
    keys = []
    for head in range(HEADS):
        at = slice(head * HD, (head + 1) * HD)
        k = _turn(projected[:, at], table_ref, 1).astype(BF16)
        out_ref[0, first, at] = k[:HALF]
        out_ref[0, second, at] = k[HALF:]
        keys.append(k)
    for copy in groups[1]:
        copy.wait()
    v = jnp.dot(x_ref[...], buffer[1], preferred_element_type=F32).astype(BF16)
    out_ref[1, first, :] = v[:HALF]
    out_ref[1, second, :] = v[HALF:]
    stat = jnp.zeros((TOK, HD), F32)
    for head in range(HEADS):
        at = slice(head * HD, (head + 1) * HD)
        peak, out = _fold(_scores(q_ref[head], keys[head]), peaks[head], v[:, at])
        out = out + part[head] * jnp.exp2(peaks[head] - peak)
        total = out[:, HD:]
        home_ref[head] = (out[:, :HD] / total).astype(BF16)
        stat = jnp.where(_lane(stat.shape) == head, peak + jnp.log2(total), stat)
    stat_ref[...] = stat


def attend_home(place, count, w, text_kv, *arrays, after):
    outs = [((2, TOK, FEAT), BF16, HBM), ((HEADS, TOK, HD), BF16), ((TOK, HD), F32)]
    scratch = [
        ((2, D, FEAT), BF16),
        (text_kv.shape, BF16),
        ((HEADS, TOK, 2 * HD), F32),
        pltpu.SemaphoreType.DMA((2 * PIECES + 1,)),
    ]
    outside = [w, text_kv]
    return kernel_call(
        _home_kernel,
        "home_attention",
        outs,
        scratch,
        [place, count],
        *arrays,
        outside=outside,
        after=after,
        limit=24,
    )


def _join_kernel(a_ref, b_ref, out_ref):
    out_ref[: MINE + 1] = a_ref[...]
    out_ref[MINE + 1 :] = b_ref[...]


def _gate_kernel(a_ref, *refs):
    del a_ref, refs


def gate(array, after):
    return pl.pallas_call(
        _gate_kernel,
        in_specs=[ANY] * (1 + len(after)),
        out_specs=ANY,
        out_shape=pltpu.VMEM(array.shape, array.dtype),
        input_output_aliases={0: 0},
        compiler_params=pltpu.CompilerParams(vmem_limit_bytes=MIB),
        cost_estimate=COST,
        name="gate",
    )(pltpu.with_memory_space_constraint(array, pltpu.VMEM), *after)


def join_units(a, b, after):
    outs = [((UNITS, TOK, HD), BF16)]
    return kernel_call(_join_kernel, "join_units", outs, [], [], a, b, after=after)[0]


def _scores(q, k):
    return lax.dot_general(q, k, (((1,), (1,)), ((), ())), preferred_element_type=F32)


def _fold(s, peak, values):
    top = s[:, :HD]
    for t in range(1, s.shape[1] // HD):
        top = jnp.maximum(top, s[:, t * HD : (t + 1) * HD])
    top = jnp.max(top, axis=1, keepdims=True)
    if peak is not None:
        top = jnp.maximum(top, peak)
    raw = jnp.exp2(s - top).astype(BF16)
    wide = jnp.concatenate([values, jnp.ones((values.shape[0], HD), BF16)], axis=1)
    return top, jnp.dot(raw, wide, preferred_element_type=F32)


def _lane(shape):
    return lax.broadcasted_iota(jnp.int32, shape, 1)


def _put(stat, u, peak, total):
    lane = _lane(stat.shape)
    return jnp.where(lane == u, peak, jnp.where(lane == u + 16, total, stat))


def _cols(index):
    return pl.ds(pl.multiple_of(index * HD, HD), HD)


def _slot_of(u, c):
    if u == MINE:
        return MINE * (1 - c)
    return (u if u < MINE else u - MINE - 1) + c


def _near_kernel(place, *refs):
    queries, keys = refs[:4], refs[4:8]
    acc_ref, stat_ref, s_ref = refs[8:]
    c = place[0]
    steps = [(u, g) for u in range(UNITS) for g in range(2)]

    def score(i):
        u, g = steps[i]
        q = jnp.concatenate([r[u, g * HALF : (g + 1) * HALF] for r in queries], axis=0)
        for b, k in enumerate(keys):
            s = _scores(q, k[0, :, _cols(_slot_of(u, c))])
            s_ref[i % 2, :, b * 2 * TOK : (b + 1) * 2 * TOK] = s
        patch = slice(0, TOK) if u <= MINE else slice(TOK, 2 * TOK)
        s_ref[i % 2, :HALF, patch] = jnp.full((HALF, TOK), -jnp.inf, F32)

    stats = [jnp.zeros((4 * HALF, HD), F32)] * 2
    score(0)
    for i, (u, g) in enumerate(steps):
        if i + 1 < len(steps):
            score(i + 1)
        values = jnp.concatenate([k[1, :, _cols(_slot_of(u, c))] for k in keys], axis=0)
        peak, out = _fold(s_ref[i % 2], None, values)
        acc_ref[u, g * 4 * HALF : (g + 1) * 4 * HALF] = out[:, :HD]
        stats[g] = _put(stats[g], u, peak, out[:, HD:])
    stat_ref[: 4 * HALF] = stats[0]
    stat_ref[4 * HALF :] = stats[1]


def attend_near(place, queries, pairs, after):
    outs = [((UNITS, 4 * TOK, HD), F32), ((4 * TOK, HD), F32)]
    scratch = [((2, 4 * HALF, 8 * TOK), F32)]
    return kernel_call(_near_kernel, "near_attention", outs, scratch, [place], *queries, *pairs, after=after)


def _far_kernel(g, place, *refs):
    queries, (acc_in, stat_in), keys = refs[:4], refs[4:6], refs[6:10]
    outs, s_ref = refs[10:14], refs[14]
    c = place[0]
    rows = slice(g * 4 * HALF, (g + 1) * 4 * HALF)

    def score(u):
        q = jnp.concatenate([r[u, g * HALF : (g + 1) * HALF] for r in queries], axis=0)
        for b, k in enumerate(keys):
            s = _scores(q, k[0, :, _cols(_slot_of(u, c))])
            s_ref[u % 2, :, b * 2 * TOK : (b + 1) * 2 * TOK] = s

    mark = jnp.zeros((4 * HALF, HD), F32)
    score(0)
    for u in range(UNITS):
        if u + 1 < UNITS:
            score(u + 1)
        before = stat_in[rows, u : u + 1]
        values = jnp.concatenate([k[1, :, _cols(_slot_of(u, c))] for k in keys], axis=0)
        peak, out = _fold(s_ref[u % 2], before, values)
        factor = jnp.exp2(before - peak)
        total = stat_in[rows, u + 16 : u + 17] * factor + out[:, HD:]
        out = ((acc_in[u, rows] * factor + out[:, :HD]) / total).astype(BF16)
        level = peak + jnp.log2(total)
        lane = _lane(level.shape)
        mark = jnp.where(lane % 16 == u, level, mark)
        for i, o in enumerate(outs):
            o[u] = out[i * HALF : (i + 1) * HALF]
    mark = _spread(mark)
    for i, o in enumerate(outs):
        o[UNITS] = mark[i * HALF : (i + 1) * HALF]


def attend_far(g, place, queries, acc, stat, pairs, after):
    outs = [((UNITS + 1, HALF, HD), BF16)] * 4
    scratch = [((2, 4 * HALF, 8 * TOK), F32)]
    kernel = functools.partial(_far_kernel, g)
    return kernel_call(kernel, f"far_attention_{g}", outs, scratch, [place], *queries, acc, stat, *pairs, after=after)


def _spread(level):
    high = level.astype(BF16).astype(F32)
    middle = (level - high).astype(BF16).astype(F32)
    lane = _lane(level.shape)
    low = level - high - middle
    return jnp.where(lane < 16, high, jnp.where(lane < 32, middle, low)).astype(BF16)


def _collect(mark):
    mark = mark.astype(F32)
    return mark + pltpu.roll(mark, HD - 16, 1) + pltpu.roll(mark, HD - 32, 1)


def _merge_kernel(p0, p1, p2, p3, mine_ref, stat_ref, sib_ref):
    parts = (p0, p1, p2, p3)
    levels = [_collect(p[UNITS]) for p in parts]
    top = functools.reduce(jnp.maximum, levels)
    weights = [jnp.exp2(v - top) for v in levels]
    total = functools.reduce(jnp.add, weights)
    weights = [w / total for w in weights]
    for u in range(UNITS):
        out = None
        for p, w in zip(parts, weights, strict=True):
            term = p[u].astype(F32) * w[:, u : u + 1]
            out = term if out is None else out + term
        if u <= MINE:
            mine_ref[u] = out.astype(BF16)
        else:
            sib_ref[u - MINE - 1] = out.astype(BF16)
    level = top + jnp.log2(total)
    stat_ref[...] = level
    lane = _lane(level.shape)
    level = jnp.where(lane < 16, level, 0.0)
    sib_ref[MINE] = _spread(level + pltpu.roll(level, 16, 1) + pltpu.roll(level, 32, 1))


def merge(parts, after):
    outs = [((MINE + 1, HALF, HD), BF16), ((HALF, HD), F32), ((MINE + 1, HALF, HD), BF16)]
    return kernel_call(_merge_kernel, "merge_parts", outs, [], [], *parts, after=after)


def _out_kernel(g, place, mine_ref, stat_ref, got_ref, home_ref, level_ref, w_ref, out_ref):
    rows = slice(g * HALF, (g + 1) * HALF)
    first = place[0] == 0
    mine = stat_ref[...]
    got = _collect(got_ref[MINE])
    attended = []
    for head in range(HEADS):
        slot = head % (MINE + 1)
        a, la = mine_ref[slot], mine[:, slot : slot + 1]
        if head != MINE:
            low = head < MINE
            b, lb = got_ref[slot], got[:, slot + MINE + 1 : slot + MINE + 2]
            a, b = (a, b) if low else (b, a)
            la, lb = (la, lb) if low else (lb, la)
            a, la = jnp.where(first, a, b), jnp.where(first, la, lb)
        h, lh = home_ref[head, rows], level_ref[rows, head : head + 1]
        top = jnp.maximum(la, lh)
        wa, wh = jnp.exp2(la - top), jnp.exp2(lh - top)
        total = wa + wh
        out = a.astype(F32) * (wa / total) + h.astype(F32) * (wh / total)
        attended.append(out.astype(BF16))
    out = jnp.dot(jnp.concatenate(attended, axis=1), w_ref[...], preferred_element_type=F32)
    out_ref[...] = out.astype(out_ref.dtype)


def project_out(g, place, kind, *arrays):
    outs = [((HALF, D), kind, HBM)]
    kernel = functools.partial(_out_kernel, g)
    return kernel_call(kernel, "output_projection", outs, [], [place], *arrays)[0]


def _bands():
    first = HD // 8
    band = (HD - first) // 2
    omega = np.repeat(10000.0 ** (-2.0 * np.arange(band // 2) / band), 2)
    along_rows = np.zeros((HD,))
    along_cols = np.zeros((HD,))
    along_rows[first : first + band] = omega
    along_cols[first + band :] = omega
    sign = np.where(np.arange(HD) % 2 == 0, -1.0, 1.0)
    return (v.astype(np.float32) for v in (along_rows, along_cols, sign))


def body(image, w_qkv, qk_gain, stale_kv, text_kv, text_count, row_offset, w_out):
    core = lax.axis_index("patch") % 2
    group = lax.axis_index("head")
    place = jnp.stack([core, group]).astype(jnp.int32)
    other_image = swap_heads(image)

    wide = (2, TOK, (MINE + 1) * HD)
    given = lax.dynamic_slice(stale_kv, (0, 0, (1 - core) * MINE * HD), wide)
    kept = lax.dynamic_slice(stale_kv, (0, 0, core * MINE * HD), wide)
    pair = jnp.concatenate([kept, move(given, _core_move)], axis=1)
    far_pair = move(pair, _y_move)
    near = [pair] + [move(pair, _key_move(d)) for d in (1, 3, 2)]

    within = jnp.arange(TOK, dtype=jnp.int32)
    within = jnp.where(within < HALF, within + (1 - group) * HALF, within - (1 - group) * HALF)
    rows = (row_offset[0] + within // COLS).astype(F32)[:, None]
    cols = (within % COLS).astype(F32)[:, None]
    along_rows, along_cols, sign = _bands()
    angles = rows * along_rows + cols * along_cols
    cosine = jnp.cos(angles)
    sine = jnp.sin(angles) * sign
    swapped = qk_gain.reshape(2, HD // 2, 2)[:, :, ::-1].reshape(2, HD)
    table = jnp.stack([qk_gain[0] * cosine, swapped[0] * sine, qk_gain[1] * cosine, swapped[1] * sine])

    w = jnp.transpose(w_qkv, (1, 0, 2))
    q_mine, q_given, q_own, x = project_queries(place, stage(w, [pair]), other_image, image, table)
    units = join_units(q_mine, move(q_given, _core_move), near[1:4])
    queries = [units] + [move(units, _query_move(d)) for d in (1, 3, 2)]
    far_pair = gate(far_pair, queries[1:4])
    far = [far_pair] + [move(far_pair, _key_move(d)) for d in (1, 3, 2)]
    acc, stat = attend_near(place, queries, near, [far_pair])
    fresh_kv, home, level = attend_home(place, text_count, w, text_kv, x, table, q_own, after=[acc])

    parts = [attend_far(g, place, queries, acc, stat, far, [home]) for g in (0, 1)]
    halves = []
    for g, kind in ((0, BF16), (1, F32)):
        back = [parts[g][0]] + [move(parts[g][i], _query_move(d)) for i, d in ((1, 3), (2, 1), (3, 2))]
        mine, mine_stat, given_back = merge(back, parts[1][:1] if g == 0 else [])
        got = move(given_back, _core_move)
        halves.append(project_out(g, place, kind, mine, mine_stat, got, home, level, w_out))
    mixed = (halves[1] + swap_heads(halves[0]).astype(F32)).astype(BF16)
    return (mixed, fresh_kv)


def solution(mesh):
    placed = (
        P(("patch", "head"), None),
        P(None, None, "head"),
        P(),
        P(None, "patch", "head"),
        P(None, None, "head"),
        P(),
        P("patch"),
        P("head", None),
    )
    return jax.shard_map(
        body,
        mesh=mesh,
        in_specs=placed,
        out_specs=(P(("patch", "head"), None), P(None, "patch", "head")),
        check_vma=False,
    )
```

```python
import functools
import math

import jax
import jax.numpy as jnp
import numpy as np
from jax import lax
from jax.experimental import pallas as pl
from jax.experimental.pallas import tpu as pltpu
from jax.sharding import PartitionSpec as P

D = 3072
HD = 128
COLS = 128
HEADS = 7
MINE = 3
UNITS = 7
TOK = 128
FEAT = HEADS * HD
HALF = TOK // 2
PIECES = 6
STEP = D // PIECES
SCALE2 = math.log2(math.e) / math.sqrt(HD)
F32 = jnp.float32
HBM = "hbm"
BF16 = jnp.bfloat16
MIB = 1024 * 1024
COST = pl.CostEstimate(flops=1, transcendentals=0, bytes_accessed=1)
SMEM = pl.BlockSpec(memory_space=pltpu.SMEM)
VMEM = pl.BlockSpec(memory_space=pltpu.VMEM)
ANY = pl.BlockSpec(memory_space=pl.ANY)


def _place(x, y, z, c):
    return ((x * 2 + y) * 4 + z) * 2 + c


def _perm(move):
    pairs = []
    for p in range(64):
        x, y, z, c = p // 16, (p // 8) % 2, (p // 2) % 4, p % 2
        pairs.append((p, _place(*move(x, y, z, c))))
    return pairs


def _key_move(d):
    return lambda x, y, z, c: ((x + d) % 4, y, z, c) if c == 0 else (x, y, (z + d) % 4, c)


def _query_move(d):
    return lambda x, y, z, c: (x, y, (z + d) % 4, c) if c == 0 else ((x + d) % 4, y, z, c)


def _core_move(x, y, z, c):
    return (x, y, z, 1 - c)


def _y_move(x, y, z, c):
    return (x, 1 - y, z, c)


def move(array, how):
    return lax.ppermute(array, "patch", _perm(how))


def swap_heads(array):
    return lax.ppermute(array, "head", [(0, 1), (1, 0)])


def kernel_call(kernel, name, out_shape, scratch_shapes, place, scalars, *arrays, after=(), outside=(), limit=12):
    scalars = [*place, *scalars]
    begin, first, count = len(place), len(scalars) + len(outside) + len(arrays), len(after)

    def run(*refs):
        head = [[ref[0] for ref in refs[:begin]]] if begin else []
        kernel(*head, *refs[begin:first], *refs[first + count :])

    return pl.pallas_call(
        run,
        in_specs=[SMEM] * len(scalars) + [ANY] * len(outside) + [VMEM] * len(arrays) + [ANY] * count,
        out_specs=[VMEM] * len(out_shape),
        out_shape=[pltpu.VMEM(*s) if len(s) == 2 else jax.ShapeDtypeStruct(*s[:2]) for s in out_shape],
        scratch_shapes=[pltpu.VMEM(*s) if isinstance(s, tuple) else s for s in scratch_shapes],
        compiler_params=pltpu.CompilerParams(vmem_limit_bytes=limit * MIB),
        cost_estimate=COST,
        name=name,
    )(*scalars, *(pltpu.with_memory_space_constraint(a, pltpu.HBM) for a in outside), *arrays, *after)


def _turn(v, table_ref, which):
    v = v * lax.rsqrt(jnp.mean(v * v, axis=-1, keepdims=True) + 1e-06)
    lane = lax.broadcasted_iota(jnp.int32, v.shape, 1)
    other = jnp.where(lane % 2 == 0, pltpu.roll(v, HD - 1, 1), pltpu.roll(v, 1, 1))
    return v * table_ref[2 * which] + other * table_ref[2 * which + 1]


def _bring(w_ref, which, out_ref, sems):
    groups = []
    for j, i in enumerate(which):
        copies = []
        for k in range(PIECES):
            rows = pl.ds(k * STEP, STEP)
            copies.append(pltpu.make_async_copy(w_ref.at[i, rows], out_ref.at[j, rows], sems.at[j * PIECES + k]))
        for copy in copies:
            copy.start()
        groups.append(copies)
    return groups


def _stage_kernel(w_ref, image_ref, out_ref, own_ref, sems, sem):
    bring = pltpu.make_async_copy(image_ref, own_ref, sem)
    bring.start()
    for copy in _bring(w_ref, (0,), out_ref, sems)[0]:
        copy.wait()
    bring.wait()


def stage(w, image, after):
    scratch = [pltpu.SemaphoreType.DMA((PIECES,)), pltpu.SemaphoreType.DMA(())]
    outs = [((1, D, FEAT), BF16), (image.shape, BF16)]
    return kernel_call(_stage_kernel, "stage", outs, scratch, [], [], outside=[w, image], after=after)


def _query_kernel(place, w_ref, oth_ref, own_ref, table_ref, qa_ref, qb_ref, q_ref, x_ref):
    x = jnp.concatenate([oth_ref[...], own_ref[...]], axis=0)
    x_ref[...] = x
    projected = jnp.dot(x, w_ref[0], preferred_element_type=F32)
    queries = []
    for head in range(HEADS):
        at = slice(head * HD, (head + 1) * HD)
        queries.append((_turn(projected[:, at], table_ref, 0) * SCALE2).astype(BF16))
        q_ref[head] = queries[head]
    qa_ref[MINE] = queries[MINE]
    first = place[0] == 0
    for i in range(MINE):
        low, high = queries[i], queries[i + MINE + 1]
        qa_ref[i] = jnp.where(first, low, high)
        qb_ref[i] = jnp.where(first, high, low)


def project_queries(place, *arrays):
    outs = [
        ((MINE + 1, TOK, HD), BF16),
        ((MINE, TOK, HD), BF16),
        ((HEADS, TOK, HD), BF16),
        ((TOK, D), BF16),
    ]
    return kernel_call(_query_kernel, "query_projection", outs, [], place, [], *arrays)


def _home_kernel(
    place, count, text_ref, w_ref, x_ref, table_ref, q_ref, out_ref, home_ref, stat_ref, text, s_ref, buffer, sem, sems
):
    bring = pltpu.make_async_copy(text_ref, text, sem)
    bring.start()
    groups = _bring(w_ref, (1, 2), buffer, sems)
    slots = text.shape[1]
    first = pl.ds(pl.multiple_of((1 - place[1]) * HALF, HALF), HALF)
    second = pl.ds(pl.multiple_of(place[1] * HALF, HALF), HALF)
    bring.wait()
    for head in range(HEADS):
        at = slice(head * HD, (head + 1) * HD)
        s = _scores(q_ref[head], text[0, :, at])
        s_ref[head, :, :slots] = jnp.where(_lane(s.shape) < count[0], s, -jnp.inf)
    for copy in groups[0]:
        copy.wait()
    projected = jnp.dot(x_ref[...], buffer[0], preferred_element_type=F32)
    for head in range(HEADS):
        at = slice(head * HD, (head + 1) * HD)
        k = _turn(projected[:, at], table_ref, 1).astype(BF16)
        out_ref[0, first, at] = k[:HALF]
        out_ref[0, second, at] = k[HALF:]
        s_ref[head, :, slots:] = _scores(q_ref[head], k)
    for copy in groups[1]:
        copy.wait()
    v = jnp.dot(x_ref[...], buffer[1], preferred_element_type=F32).astype(BF16)
    out_ref[1, first, :] = v[:HALF]
    out_ref[1, second, :] = v[HALF:]
    stat = jnp.zeros((TOK, HD), F32)
    for head in range(HEADS):
        at = slice(head * HD, (head + 1) * HD)
        peak, out = _fold(s_ref[head], None, jnp.concatenate([text[1, :, at], v[:, at]], axis=0))
        total = out[:, HD:]
        home_ref[head] = (out[:, :HD] / total).astype(BF16)
        stat = jnp.where(_lane(stat.shape) == head, peak + jnp.log2(total), stat)
    stat_ref[...] = stat


def attend_home(place, count, text_kv, w, *arrays, after):
    outs = [((2, TOK, FEAT), BF16, HBM), ((HEADS, TOK, HD), BF16), ((TOK, HD), F32)]
    scratch = [
        (text_kv.shape, BF16),
        ((HEADS, TOK, text_kv.shape[1] + TOK), F32),
        ((2, D, FEAT), BF16),
        pltpu.SemaphoreType.DMA(()),
        pltpu.SemaphoreType.DMA((2 * PIECES,)),
    ]
    return kernel_call(
        _home_kernel,
        "home_attention",
        outs,
        scratch,
        place,
        [count],
        *arrays,
        outside=[text_kv, w],
        after=after,
        limit=24,
    )


def _join_kernel(a_ref, b_ref, out_ref):
    out_ref[: MINE + 1] = a_ref[...]
    out_ref[MINE + 1 :] = b_ref[...]


def _gate_kernel(a_ref, *refs):
    del a_ref, refs


def gate(array, after):
    return pl.pallas_call(
        _gate_kernel,
        in_specs=[ANY] * (1 + len(after)),
        out_specs=ANY,
        out_shape=pltpu.VMEM(array.shape, array.dtype),
        input_output_aliases={0: 0},
        compiler_params=pltpu.CompilerParams(vmem_limit_bytes=MIB),
        cost_estimate=COST,
        name="gate",
    )(pltpu.with_memory_space_constraint(array, pltpu.VMEM), *after)


def join_units(a, b, after):
    outs = [((UNITS, TOK, HD), BF16)]
    return kernel_call(_join_kernel, "join_units", outs, [], [], [], a, b, after=after)[0]


def _scores(q, k):
    return lax.dot_general(q, k, (((1,), (1,)), ((), ())), preferred_element_type=F32)


def _fold(s, peak, values):
    top = s[:, :HD]
    for t in range(1, s.shape[1] // HD):
        top = jnp.maximum(top, s[:, t * HD : (t + 1) * HD])
    top = jnp.max(top, axis=1, keepdims=True)
    if peak is not None:
        top = jnp.maximum(top, peak)
    raw = jnp.exp2(s - top).astype(BF16)
    wide = jnp.concatenate([values, jnp.ones((values.shape[0], HD), BF16)], axis=1)
    return top, jnp.dot(raw, wide, preferred_element_type=F32)


def _lane(shape):
    return lax.broadcasted_iota(jnp.int32, shape, 1)


def _put(stat, u, peak, total):
    lane = _lane(stat.shape)
    return jnp.where(lane == u, peak, jnp.where(lane == u + 16, total, stat))


def _cols(index):
    return pl.ds(pl.multiple_of(index * HD, HD), HD)


def _slot_of(u, c):
    if u == MINE:
        return MINE * (1 - c)
    return (u if u < MINE else u - MINE - 1) + c


ORDER = ((1, 2, 3, 0), (0, 1, 2, 3))
OWN = (slice(3 * HALF, 4 * HALF), slice(0, HALF))
ROWS = (((1, 0), (2, 0), (3, 0)), ((0, 0), (0, 1), (1, 1), (2, 1), (3, 1)))


def _gather(refs, u, rows):
    return jnp.concatenate([refs[i][u, g * HALF : (g + 1) * HALF] for i, g in rows], axis=0)


def _near_kernel(place, *refs):
    queries, keys = refs[:4], refs[4:8]
    acc_ref, stat_ref, s_ref = refs[8:]
    c = place[0]
    steps = [(u, g) for u in range(UNITS) for g in range(2)]

    def score(i):
        u, g = steps[i]
        q = _gather(queries, u, [(r, g) for r in ORDER[g]])
        for b, k in enumerate(keys):
            s = _scores(q, k[0, :, _cols(_slot_of(u, c))])
            s_ref[i % 2, :, b * 2 * TOK : (b + 1) * 2 * TOK] = s
        patch = slice(0, TOK) if u <= MINE else slice(TOK, 2 * TOK)
        s_ref[i % 2, OWN[g], patch] = jnp.full((HALF, TOK), -jnp.inf, F32)

    stats = [jnp.zeros((4 * HALF, HD), F32)] * 2
    score(0)
    for i, (u, g) in enumerate(steps):
        if i + 1 < len(steps):
            score(i + 1)
        values = jnp.concatenate([k[1, :, _cols(_slot_of(u, c))] for k in keys], axis=0)
        peak, out = _fold(s_ref[i % 2], None, values)
        acc_ref[u, g * 4 * HALF : (g + 1) * 4 * HALF] = out[:, :HD]
        stats[g] = _put(stats[g], u, peak, out[:, HD:])
    stat_ref[: 4 * HALF] = stats[0]
    stat_ref[4 * HALF :] = stats[1]


def attend_near(place, queries, pairs, after):
    outs = [((UNITS, 4 * TOK, HD), F32), ((4 * TOK, HD), F32)]
    scratch = [((2, 4 * HALF, 8 * TOK), F32)]
    return kernel_call(_near_kernel, "near_attention", outs, scratch, place, [], *queries, *pairs, after=after)


def _far_kernel(g, place, *refs):
    queries, (acc_in, stat_in), keys = refs[:4], refs[4:6], refs[6:10]
    outs, s_ref = refs[10:-1], refs[-1]
    c = place[0]
    count = len(ROWS[g]) * HALF
    rows = slice(0, count) if g == 0 else slice(4 * TOK - count, 4 * TOK)

    def score(u):
        q = _gather(queries, u, ROWS[g])
        for b, k in enumerate(keys):
            s = _scores(q, k[0, :, _cols(_slot_of(u, c))])
            s_ref[u % 2, :, b * 2 * TOK : (b + 1) * 2 * TOK] = s

    mark = jnp.zeros((count, HD), F32)
    score(0)
    for u in range(UNITS):
        if u + 1 < UNITS:
            score(u + 1)
        before = stat_in[rows, u : u + 1]
        values = jnp.concatenate([k[1, :, _cols(_slot_of(u, c))] for k in keys], axis=0)
        peak, out = _fold(s_ref[u % 2], before, values)
        factor = jnp.exp2(before - peak)
        total = stat_in[rows, u + 16 : u + 17] * factor + out[:, HD:]
        out = ((acc_in[u, rows] * factor + out[:, :HD]) / total).astype(BF16)
        level = peak + jnp.log2(total)
        mark = jnp.where(_lane(level.shape) % 16 == u, level, mark)
        _deal(outs, u, out)
    _deal(outs, UNITS, _spread(mark))


def _deal(outs, u, rows):
    at = 0
    for o in outs:
        o[u] = rows[at : at + o.shape[1]]
        at += o.shape[1]


def attend_far(g, place, queries, acc, stat, pairs, after):
    outs = [((UNITS + 1, HALF, HD), BF16)] * 3
    if g == 1:
        outs = [((UNITS + 1, TOK, HD), BF16)] + outs
    scratch = [((2, len(ROWS[g]) * HALF, 8 * TOK), F32)]
    kernel = functools.partial(_far_kernel, g)
    arrays = (*queries, acc, stat, *pairs)
    return kernel_call(kernel, f"far_attention_{g}", outs, scratch, place, [], *arrays, after=after)


def _spread(level):
    high = level.astype(BF16).astype(F32)
    middle = (level - high).astype(BF16).astype(F32)
    lane = _lane(level.shape)
    low = level - high - middle
    return jnp.where(lane < 16, high, jnp.where(lane < 32, middle, low)).astype(BF16)


def _collect(mark):
    mark = mark.astype(F32)
    return mark + pltpu.roll(mark, HD - 16, 1) + pltpu.roll(mark, HD - 32, 1)


def _merge_kernel(g, p0, p1, p2, p3, mine_ref, stat_ref, sib_ref):
    parts = (p0.at[:, g * HALF : (g + 1) * HALF], p1, p2, p3)
    levels = [_collect(p[UNITS]) for p in parts]
    top = functools.reduce(jnp.maximum, levels)
    weights = [jnp.exp2(v - top) for v in levels]
    total = functools.reduce(jnp.add, weights)
    weights = [w / total for w in weights]
    for u in range(UNITS):
        out = None
        for p, w in zip(parts, weights, strict=True):
            term = p[u].astype(F32) * w[:, u : u + 1]
            out = term if out is None else out + term
        if u <= MINE:
            mine_ref[u] = out.astype(BF16)
        else:
            sib_ref[u - MINE - 1] = out.astype(BF16)
    level = top + jnp.log2(total)
    stat_ref[...] = level
    lane = _lane(level.shape)
    level = jnp.where(lane < 16, level, 0.0)
    sib_ref[MINE] = _spread(level + pltpu.roll(level, 16, 1) + pltpu.roll(level, 32, 1))


def merge(g, parts):
    outs = [((MINE + 1, HALF, HD), BF16), ((HALF, HD), F32), ((MINE + 1, HALF, HD), BF16)]
    return kernel_call(functools.partial(_merge_kernel, g), "merge_parts", outs, [], [], [], *parts)


def _out_kernel(g, place, mine_ref, stat_ref, got_ref, home_ref, level_ref, w_ref, *rest):
    *other, out_ref = rest
    rows = slice(g * HALF, (g + 1) * HALF)
    first = place[0] == 0
    mine = stat_ref[...]
    got = _collect(got_ref[MINE])
    attended = []
    for head in range(HEADS):
        slot = head % (MINE + 1)
        a, la = mine_ref[slot], mine[:, slot : slot + 1]
        if head != MINE:
            low = head < MINE
            b, lb = got_ref[slot], got[:, slot + MINE + 1 : slot + MINE + 2]
            a, b = (a, b) if low else (b, a)
            la, lb = (la, lb) if low else (lb, la)
            a, la = jnp.where(first, a, b), jnp.where(first, la, lb)
        h, lh = home_ref[head, rows], level_ref[rows, head : head + 1]
        top = jnp.maximum(la, lh)
        wa, wh = jnp.exp2(la - top), jnp.exp2(lh - top)
        total = wa + wh
        out = a.astype(F32) * (wa / total) + h.astype(F32) * (wh / total)
        attended.append(out.astype(BF16))
    out = jnp.dot(jnp.concatenate(attended, axis=1), w_ref[...], preferred_element_type=F32)
    for ref in other:
        out = out + ref[...].astype(F32)
    out_ref[...] = out.astype(BF16)


def project_out(g, place, *arrays, after):
    outs = [((HALF, D), BF16, HBM)]
    kernel = functools.partial(_out_kernel, g)
    return kernel_call(kernel, "output_projection", outs, [], place, [], *arrays, after=after)[0]


def _bands():
    first = HD // 8
    band = (HD - first) // 2
    omega = np.repeat(10000.0 ** (-2.0 * np.arange(band // 2) / band), 2)
    along_rows = np.zeros((HD,))
    along_cols = np.zeros((HD,))
    along_rows[first : first + band] = omega
    along_cols[first + band :] = omega
    sign = np.where(np.arange(HD) % 2 == 0, -1.0, 1.0)
    return (v.astype(np.float32) for v in (along_rows, along_cols, sign))


def body(image, w_qkv, qk_gain, stale_kv, text_kv, text_count, row_offset, w_out):
    core = lax.axis_index("patch") % 2
    group = lax.axis_index("head")
    place = [core.astype(jnp.int32).reshape(1), group.astype(jnp.int32).reshape(1)]
    other_image = swap_heads(image)

    wide = (2, TOK, (MINE + 1) * HD)
    given = lax.dynamic_slice(stale_kv, (0, 0, (1 - core) * MINE * HD), wide)
    kept = lax.dynamic_slice(stale_kv, (0, 0, core * MINE * HD), wide)
    pair = jnp.concatenate([kept, move(given, _core_move)], axis=1)
    far_pair = move(pair, _y_move)
    near = [pair] + [move(pair, _key_move(d)) for d in (1, 3, 2)]

    within = jnp.arange(TOK, dtype=jnp.int32)
    within = jnp.where(within < HALF, within + (1 - group) * HALF, within - (1 - group) * HALF)
    rows = (row_offset[0] + within // COLS).astype(F32)[:, None]
    cols = (within % COLS).astype(F32)[:, None]
    along_rows, along_cols, sign = _bands()
    angles = rows * along_rows + cols * along_cols
    cosine = jnp.cos(angles)
    sine = jnp.sin(angles) * sign
    swapped = qk_gain.reshape(2, HD // 2, 2)[:, :, ::-1].reshape(2, HD)
    table = jnp.stack([qk_gain[0] * cosine, swapped[0] * sine, qk_gain[1] * cosine, swapped[1] * sine])

    w = jnp.transpose(w_qkv, (1, 0, 2))
    staged, own_image = stage(w, image, [pair])
    q_mine, q_given, q_own, x = project_queries(place, staged, other_image, own_image, table)
    units = join_units(q_mine, move(q_given, _core_move), near[1:3])
    queries = [units] + [move(units, _query_move(d)) for d in (1, 3, 2)]
    far_two = move(near[3], _y_move)
    fresh_kv, home, level = attend_home(place, text_count, text_kv, w, x, table, q_own, after=[units, near[3]])
    far_pair = gate(far_pair, queries[1:4] + [home])
    far = [far_pair] + [move(far_pair, _key_move(d)) for d in (1, 3)] + [far_two]
    acc, stat = attend_near(place, queries, near, [far_pair])

    first = attend_far(0, place, queries, acc, stat, far, [])
    own, *second = attend_far(1, place, queries, acc, stat, far, [])
    back = [[own] + [move(p, _query_move(d)) for p, d in zip(parts, (3, 1, 2))] for parts in (first, second)]
    merged = [merge(g, back[g]) for g in (0, 1)]
    got = [move(merged[g][2], _core_move) for g in (0, 1)]
    sent = project_out(0, place, *merged[0][:2], got[0], home, level, w_out, after=[])
    mixed = project_out(1, place, *merged[1][:2], got[1], home, level, w_out, swap_heads(sent), after=[])
    return (mixed, fresh_kv)


def solution(mesh):
    placed = (
        P(("patch", "head"), None),
        P(None, None, "head"),
        P(),
        P(None, "patch", "head"),
        P(None, None, "head"),
        P(),
        P("patch"),
        P("head", None),
    )
    return jax.shard_map(
        body,
        mesh=mesh,
        in_specs=placed,
        out_specs=(P(("patch", "head"), None), P(None, "patch", "head")),
        check_vma=False,
    )
```

```python
import functools
import math

import jax
import jax.numpy as jnp
import numpy as np
from jax import lax
from jax.experimental import pallas as pl
from jax.experimental.pallas import tpu as pltpu
from jax.sharding import PartitionSpec as P

D = 3072
HD = 128
COLS = 128
HEADS = 7
MINE = 3
UNITS = 7
TOK = 128
FEAT = HEADS * HD
HALF = TOK // 2
PIECES = 6
STEP = D // PIECES
SCALE2 = math.log2(math.e) / math.sqrt(HD)
F32 = jnp.float32
HBM = "hbm"
BF16 = jnp.bfloat16
MIB = 1024 * 1024
COST = pl.CostEstimate(flops=1, transcendentals=0, bytes_accessed=1)
SMEM = pl.BlockSpec(memory_space=pltpu.SMEM)
VMEM = pl.BlockSpec(memory_space=pltpu.VMEM)
ANY = pl.BlockSpec(memory_space=pl.ANY)


def _place(x, y, z, c):
    return ((x * 2 + y) * 4 + z) * 2 + c


def _perm(move):
    pairs = []
    for p in range(64):
        x, y, z, c = p // 16, (p // 8) % 2, (p // 2) % 4, p % 2
        pairs.append((p, _place(*move(x, y, z, c))))
    return pairs


def _key_move(d):
    return lambda x, y, z, c: ((x + d) % 4, y, z, c) if c == 0 else (x, y, (z + d) % 4, c)


def _query_move(d):
    return lambda x, y, z, c: (x, y, (z + d) % 4, c) if c == 0 else ((x + d) % 4, y, z, c)


def _core_move(x, y, z, c):
    return (x, y, z, 1 - c)


def _y_move(x, y, z, c):
    return (x, 1 - y, z, c)


def move(array, how):
    return lax.ppermute(array, "patch", _perm(how))


def swap_heads(array):
    return lax.ppermute(array, "head", [(0, 1), (1, 0)])


def kernel_call(kernel, name, out_shape, scratch_shapes, place, scalars, *arrays, after=(), outside=(), limit=12):
    scalars = [*place, *scalars]
    begin, first, count = len(place), len(scalars) + len(outside) + len(arrays), len(after)

    def run(*refs):
        head = [[ref[0] for ref in refs[:begin]]] if begin else []
        kernel(*head, *refs[begin:first], *refs[first + count :])

    return pl.pallas_call(
        run,
        in_specs=[SMEM] * len(scalars) + [ANY] * len(outside) + [VMEM] * len(arrays) + [ANY] * count,
        out_specs=[VMEM] * len(out_shape),
        out_shape=[pltpu.VMEM(*s) if len(s) == 2 else jax.ShapeDtypeStruct(*s[:2]) for s in out_shape],
        scratch_shapes=[pltpu.VMEM(*s) if isinstance(s, tuple) else s for s in scratch_shapes],
        compiler_params=pltpu.CompilerParams(vmem_limit_bytes=limit * MIB),
        cost_estimate=COST,
        name=name,
    )(*scalars, *(pltpu.with_memory_space_constraint(a, pltpu.HBM) for a in outside), *arrays, *after)


def _turn(v, table_ref, which):
    v = v * lax.rsqrt(jnp.mean(v * v, axis=-1, keepdims=True) + 1e-06)
    lane = lax.broadcasted_iota(jnp.int32, v.shape, 1)
    other = jnp.where(lane % 2 == 0, pltpu.roll(v, HD - 1, 1), pltpu.roll(v, 1, 1))
    return v * table_ref[2 * which] + other * table_ref[2 * which + 1]


def _bring(w_ref, which, out_ref, sems):
    groups = []
    for j, i in enumerate(which):
        copies = []
        for k in range(PIECES):
            rows = pl.ds(k * STEP, STEP)
            copies.append(pltpu.make_async_copy(w_ref.at[i, rows], out_ref.at[j, rows], sems.at[j * PIECES + k]))
        for copy in copies:
            copy.start()
        groups.append(copies)
    return groups


def _stage_kernel(w_ref, image_ref, g_ref, turn_ref, out_ref, own_ref, table_ref, gain_ref, sems, more):
    copies = _bring(w_ref, (0,), out_ref, sems)[0]
    small = [pltpu.make_async_copy(g_ref, gain_ref, more.at[0]), pltpu.make_async_copy(image_ref, own_ref, more.at[1])]
    for copy in small:
        copy.start()
    small[0].wait()
    even = _lane((8, HD)) % 2 == 0
    for i in range(2):
        gain = jnp.broadcast_to(gain_ref[i : i + 1, :], (8, HD))
        swapped = jnp.where(even, pltpu.roll(gain, HD - 1, 1), pltpu.roll(gain, 1, 1))
        table_ref[2 * i] = turn_ref[0] * gain[0:1]
        table_ref[2 * i + 1] = turn_ref[1] * swapped[0:1]
    for copy in copies:
        copy.wait()
    small[1].wait()


def stage(w, image, gain, turns, after):
    scratch = [((2, HD), F32), pltpu.SemaphoreType.DMA((PIECES,)), pltpu.SemaphoreType.DMA((2,))]
    outs = [((1, D, FEAT), BF16), (image.shape, BF16), ((4, TOK, HD), F32)]
    return kernel_call(_stage_kernel, "stage", outs, scratch, [], [], turns, outside=[w, image, gain], after=after)


def _query_kernel(place, w_ref, oth_ref, own_ref, table_ref, qa_ref, qb_ref, q_ref, x_ref):
    x = jnp.concatenate([oth_ref[...], own_ref[...]], axis=0)
    x_ref[...] = x
    projected = jnp.dot(x, w_ref[0], preferred_element_type=F32)
    queries = []
    for head in range(HEADS):
        at = slice(head * HD, (head + 1) * HD)
        queries.append((_turn(projected[:, at], table_ref, 0) * SCALE2).astype(BF16))
        q_ref[head] = queries[head]
    qa_ref[MINE] = queries[MINE]
    first = place[0] == 0
    for i in range(MINE):
        low, high = queries[i], queries[i + MINE + 1]
        qa_ref[i] = jnp.where(first, low, high)
        qb_ref[i] = jnp.where(first, high, low)


def project_queries(place, *arrays):
    outs = [
        ((MINE + 1, TOK, HD), BF16),
        ((MINE, TOK, HD), BF16),
        ((HEADS, TOK, HD), BF16),
        ((TOK, D), BF16),
    ]
    return kernel_call(_query_kernel, "query_projection", outs, [], place, [], *arrays)


def _home_kernel(
    place, count, text_ref, w_ref, x_ref, table_ref, q_ref, out_ref, home_ref, stat_ref, text, s_ref, sem
):
    bring = pltpu.make_async_copy(text_ref, text, sem)
    bring.start()
    slots = text.shape[1]
    first = pl.ds(pl.multiple_of((1 - place[1]) * HALF, HALF), HALF)
    second = pl.ds(pl.multiple_of(place[1] * HALF, HALF), HALF)
    bring.wait()
    for head in range(HEADS):
        at = slice(head * HD, (head + 1) * HD)
        s = _scores(q_ref[head], text[0, :, at])
        s_ref[head, :, :slots] = jnp.where(_lane(s.shape) < count[0], s, -jnp.inf)
    projected = jnp.dot(x_ref[...], w_ref[1], preferred_element_type=F32)
    for head in range(HEADS):
        at = slice(head * HD, (head + 1) * HD)
        k = _turn(projected[:, at], table_ref, 1).astype(BF16)
        out_ref[0, first, at] = k[:HALF]
        out_ref[0, second, at] = k[HALF:]
        s_ref[head, :, slots:] = _scores(q_ref[head], k)
    v = jnp.dot(x_ref[...], w_ref[2], preferred_element_type=F32).astype(BF16)
    out_ref[1, first, :] = v[:HALF]
    out_ref[1, second, :] = v[HALF:]
    stat = jnp.zeros((TOK, HD), F32)
    for head in range(HEADS):
        at = slice(head * HD, (head + 1) * HD)
        peak, out = _fold(s_ref[head], None, jnp.concatenate([text[1, :, at], v[:, at]], axis=0))
        total = out[:, HD:]
        home_ref[head] = (out[:, :HD] / total).astype(BF16)
        stat = jnp.where(_lane(stat.shape) == head, peak + jnp.log2(total), stat)
    stat_ref[...] = stat


def attend_home(place, count, text_kv, w, *arrays, after):
    outs = [((2, TOK, FEAT), BF16, HBM), ((HEADS, TOK, HD), BF16), ((TOK, HD), F32)]
    scratch = [
        (text_kv.shape, BF16),
        ((HEADS, TOK, text_kv.shape[1] + TOK), F32),
        pltpu.SemaphoreType.DMA(()),
    ]
    return kernel_call(
        _home_kernel,
        "home_attention",
        outs,
        scratch,
        place,
        [count],
        w,
        *arrays,
        outside=[text_kv],
        after=after,
        limit=12,
    )


def _join_kernel(a_ref, b_ref, out_ref):
    out_ref[: MINE + 1] = a_ref[...]
    out_ref[MINE + 1 :] = b_ref[...]


def _gate_kernel(a_ref, *refs):
    del a_ref, refs


def gate(array, after):
    return pl.pallas_call(
        _gate_kernel,
        in_specs=[ANY] * (1 + len(after)),
        out_specs=ANY,
        out_shape=pltpu.VMEM(array.shape, array.dtype),
        input_output_aliases={0: 0},
        compiler_params=pltpu.CompilerParams(vmem_limit_bytes=MIB),
        cost_estimate=COST,
        name="gate",
    )(pltpu.with_memory_space_constraint(array, pltpu.VMEM), *after)


def join_units(a, b, after):
    outs = [((UNITS, TOK, HD), BF16)]
    return kernel_call(_join_kernel, "join_units", outs, [], [], [], a, b, after=after)[0]


def _scores(q, k):
    return lax.dot_general(q, k, (((1,), (1,)), ((), ())), preferred_element_type=F32)


def _fold(s, peak, values):
    top = s[:, :HD]
    for t in range(1, s.shape[1] // HD):
        top = jnp.maximum(top, s[:, t * HD : (t + 1) * HD])
    top = jnp.max(top, axis=1, keepdims=True)
    if peak is not None:
        top = jnp.maximum(top, peak)
    raw = jnp.exp2(s - top).astype(BF16)
    wide = jnp.concatenate([values, jnp.ones((values.shape[0], HD), BF16)], axis=1)
    return top, jnp.dot(raw, wide, preferred_element_type=F32)


def _lane(shape):
    return lax.broadcasted_iota(jnp.int32, shape, 1)


def _put(stat, u, peak, total):
    lane = _lane(stat.shape)
    return jnp.where(lane == u, peak, jnp.where(lane == u + 16, total, stat))


def _cols(index):
    return pl.ds(pl.multiple_of(index * HD, HD), HD)


def _slot_of(u, c):
    if u == MINE:
        return MINE * (1 - c)
    return (u if u < MINE else u - MINE - 1) + c


ORDER = ((1, 2, 3, 0), (0, 1, 2, 3))
OWN = (slice(3 * HALF, 4 * HALF), slice(0, HALF))
ROWS = (((1, 0), (2, 0), (3, 0)), ((0, 0), (0, 1), (1, 1), (2, 1), (3, 1)))


def _gather(refs, u, rows):
    return jnp.concatenate([refs[i][u, g * HALF : (g + 1) * HALF] for i, g in rows], axis=0)


def _near_kernel(place, *refs):
    queries, keys = refs[:4], refs[4:8]
    acc_ref, stat_ref, s_ref = refs[8:]
    c = place[0]
    steps = [(u, g) for u in range(UNITS) for g in range(2)]

    def score(i):
        u, g = steps[i]
        q = _gather(queries, u, [(r, g) for r in ORDER[g]])
        for b, k in enumerate(keys):
            s = _scores(q, k[0, :, _cols(_slot_of(u, c))])
            s_ref[i % 2, :, b * 2 * TOK : (b + 1) * 2 * TOK] = s
        patch = slice(0, TOK) if u <= MINE else slice(TOK, 2 * TOK)
        s_ref[i % 2, OWN[g], patch] = jnp.full((HALF, TOK), -jnp.inf, F32)

    stats = [jnp.zeros((4 * HALF, HD), F32)] * 2
    score(0)
    for i, (u, g) in enumerate(steps):
        if i + 1 < len(steps):
            score(i + 1)
        values = jnp.concatenate([k[1, :, _cols(_slot_of(u, c))] for k in keys], axis=0)
        peak, out = _fold(s_ref[i % 2], None, values)
        acc_ref[u, g * 4 * HALF : (g + 1) * 4 * HALF] = out[:, :HD]
        stats[g] = _put(stats[g], u, peak, out[:, HD:])
    stat_ref[: 4 * HALF] = stats[0]
    stat_ref[4 * HALF :] = stats[1]


def attend_near(place, queries, pairs, after):
    outs = [((UNITS, 4 * TOK, HD), F32), ((4 * TOK, HD), F32)]
    scratch = [((2, 4 * HALF, 8 * TOK), F32)]
    return kernel_call(_near_kernel, "near_attention", outs, scratch, place, [], *queries, *pairs, after=after)


def _far_kernel(g, place, *refs):
    queries, (acc_in, stat_in), keys = refs[:4], refs[4:6], refs[6:10]
    outs, s_ref = refs[10:-1], refs[-1]
    c = place[0]
    count = len(ROWS[g]) * HALF
    rows = slice(0, count) if g == 0 else slice(4 * TOK - count, 4 * TOK)

    def score(u):
        q = _gather(queries, u, ROWS[g])
        for b, k in enumerate(keys):
            s = _scores(q, k[0, :, _cols(_slot_of(u, c))])
            s_ref[u % 2, :, b * 2 * TOK : (b + 1) * 2 * TOK] = s

    mark = jnp.zeros((count, HD), F32)
    score(0)
    for u in range(UNITS):
        if u + 1 < UNITS:
            score(u + 1)
        before = stat_in[rows, u : u + 1]
        values = jnp.concatenate([k[1, :, _cols(_slot_of(u, c))] for k in keys], axis=0)
        peak, out = _fold(s_ref[u % 2], before, values)
        factor = jnp.exp2(before - peak)
        total = stat_in[rows, u + 16 : u + 17] * factor + out[:, HD:]
        out = ((acc_in[u, rows] * factor + out[:, :HD]) / total).astype(BF16)
        level = peak + jnp.log2(total)
        mark = jnp.where(_lane(level.shape) % 16 == u, level, mark)
        _deal(outs, u, out)
    _deal(outs, UNITS, _spread(mark))


def _deal(outs, u, rows):
    at = 0
    for o in outs:
        o[u] = rows[at : at + o.shape[1]]
        at += o.shape[1]


def attend_far(g, place, queries, acc, stat, pairs, after):
    outs = [((UNITS + 1, HALF, HD), BF16)] * 3
    if g == 1:
        outs = [((UNITS + 1, TOK, HD), BF16)] + outs
    scratch = [((2, len(ROWS[g]) * HALF, 8 * TOK), F32)]
    kernel = functools.partial(_far_kernel, g)
    arrays = (*queries, acc, stat, *pairs)
    return kernel_call(kernel, f"far_attention_{g}", outs, scratch, place, [], *arrays, after=after)


def _spread(level):
    high = level.astype(BF16).astype(F32)
    middle = (level - high).astype(BF16).astype(F32)
    lane = _lane(level.shape)
    low = level - high - middle
    return jnp.where(lane < 16, high, jnp.where(lane < 32, middle, low)).astype(BF16)


def _collect(mark):
    mark = mark.astype(F32)
    return mark + pltpu.roll(mark, HD - 16, 1) + pltpu.roll(mark, HD - 32, 1)


def _merge_kernel(g, p0, p1, p2, p3, mine_ref, stat_ref, sib_ref):
    parts = (p0.at[:, g * HALF : (g + 1) * HALF], p1, p2, p3)
    levels = [_collect(p[UNITS]) for p in parts]
    top = functools.reduce(jnp.maximum, levels)
    weights = [jnp.exp2(v - top) for v in levels]
    total = functools.reduce(jnp.add, weights)
    weights = [w / total for w in weights]
    for u in range(UNITS):
        out = None
        for p, w in zip(parts, weights, strict=True):
            term = p[u].astype(F32) * w[:, u : u + 1]
            out = term if out is None else out + term
        if u <= MINE:
            mine_ref[u] = out.astype(BF16)
        else:
            sib_ref[u - MINE - 1] = out.astype(BF16)
    level = top + jnp.log2(total)
    stat_ref[...] = level
    lane = _lane(level.shape)
    level = jnp.where(lane < 16, level, 0.0)
    sib_ref[MINE] = _spread(level + pltpu.roll(level, 16, 1) + pltpu.roll(level, 32, 1))


def merge(g, parts):
    outs = [((MINE + 1, HALF, HD), BF16), ((HALF, HD), F32), ((MINE + 1, HALF, HD), BF16)]
    return kernel_call(functools.partial(_merge_kernel, g), "merge_parts", outs, [], [], [], *parts)


def _out_kernel(g, place, mine_ref, stat_ref, got_ref, home_ref, level_ref, w_ref, *rest):
    *other, out_ref = rest
    rows = slice(g * HALF, (g + 1) * HALF)
    first = place[0] == 0
    mine = stat_ref[...]
    got = _collect(got_ref[MINE])
    attended = []
    for head in range(HEADS):
        slot = head % (MINE + 1)
        a, la = mine_ref[slot], mine[:, slot : slot + 1]
        if head != MINE:
            low = head < MINE
            b, lb = got_ref[slot], got[:, slot + MINE + 1 : slot + MINE + 2]
            a, b = (a, b) if low else (b, a)
            la, lb = (la, lb) if low else (lb, la)
            a, la = jnp.where(first, a, b), jnp.where(first, la, lb)
        h, lh = home_ref[head, rows], level_ref[rows, head : head + 1]
        top = jnp.maximum(la, lh)
        wa, wh = jnp.exp2(la - top), jnp.exp2(lh - top)
        total = wa + wh
        out = a.astype(F32) * (wa / total) + h.astype(F32) * (wh / total)
        attended.append(out.astype(BF16))
    out = jnp.dot(jnp.concatenate(attended, axis=1), w_ref[...], preferred_element_type=F32)
    for ref in other:
        out = out + ref[...].astype(F32)
    out_ref[...] = out.astype(BF16)


def project_out(g, place, *arrays, after):
    outs = [((HALF, D), BF16, HBM)]
    kernel = functools.partial(_out_kernel, g)
    return kernel_call(kernel, "output_projection", outs, [], place, [], *arrays, after=after)[0]


def _bands():
    first = HD // 8
    band = (HD - first) // 2
    omega = np.repeat(10000.0 ** (-2.0 * np.arange(band // 2) / band), 2)
    along_rows = np.zeros((HD,))
    along_cols = np.zeros((HD,))
    along_rows[first : first + band] = omega
    along_cols[first + band :] = omega
    sign = np.where(np.arange(HD) % 2 == 0, -1.0, 1.0)
    return (v.astype(np.float32) for v in (along_rows, along_cols, sign))


def body(image, w_qkv, qk_gain, stale_kv, text_kv, text_count, row_offset, w_out):
    core = lax.axis_index("patch") % 2
    group = lax.axis_index("head")
    place = [core.astype(jnp.int32).reshape(1), group.astype(jnp.int32).reshape(1)]
    other_image = swap_heads(image)

    wide = (2, TOK, (MINE + 1) * HD)
    given = lax.dynamic_slice(stale_kv, (0, 0, (1 - core) * MINE * HD), wide)
    kept = lax.dynamic_slice(stale_kv, (0, 0, core * MINE * HD), wide)
    pair = jnp.concatenate([kept, move(given, _core_move)], axis=1)
    far_pair = move(pair, _y_move)
    near = [pair] + [move(pair, _key_move(d)) for d in (1, 3, 2)]

    within = jnp.arange(TOK, dtype=jnp.int32)
    within = jnp.where(within < HALF, within + (1 - group) * HALF, within - (1 - group) * HALF)
    rows = (row_offset[0] + within // COLS).astype(F32)[:, None]
    cols = (within % COLS).astype(F32)[:, None]
    along_rows, along_cols, sign = _bands()
    angles = rows * along_rows + cols * along_cols
    turns = jnp.stack([jnp.cos(angles), jnp.sin(angles) * sign])

    w = jnp.transpose(w_qkv, (1, 0, 2))
    staged, own_image, table = stage(w, image, qk_gain, turns, [pair])
    q_mine, q_given, q_own, x = project_queries(place, staged, other_image, own_image, table)
    units = join_units(q_mine, move(q_given, _core_move), near[1:3])
    queries = [units] + [move(units, _query_move(d)) for d in (1, 3, 2)]
    far_two = move(near[3], _y_move)
    fresh_kv, home, level = attend_home(place, text_count, text_kv, w, x, table, q_own, after=[units, near[3]])
    far_pair = gate(far_pair, queries[1:4] + [home])
    far = [far_pair] + [move(far_pair, _key_move(d)) for d in (1, 3)] + [far_two]
    acc, stat = attend_near(place, queries, near, [far_pair])

    first = attend_far(0, place, queries, acc, stat, far, [])
    own, *second = attend_far(1, place, queries, acc, stat, far, [])
    back = [[own] + [move(p, _query_move(d)) for p, d in zip(parts, (3, 1, 2))] for parts in (first, second)]
    merged = [merge(g, back[g]) for g in (0, 1)]
    got = [move(merged[g][2], _core_move) for g in (0, 1)]
    sent = project_out(0, place, *merged[0][:2], got[0], home, level, w_out, after=[])
    mixed = project_out(1, place, *merged[1][:2], got[1], home, level, w_out, swap_heads(sent), after=[])
    return (mixed, fresh_kv)


def solution(mesh):
    placed = (
        P(("patch", "head"), None),
        P(None, None, "head"),
        P(),
        P(None, "patch", "head"),
        P(None, None, "head"),
        P(),
        P("patch"),
        P("head", None),
    )
    return jax.shard_map(
        body,
        mesh=mesh,
        in_specs=placed,
        out_specs=(P(("patch", "head"), None), P(None, "patch", "head")),
        check_vma=False,
    )
```

```python
import functools
import math

import jax
import jax.numpy as jnp
import numpy as np
from jax import lax
from jax.experimental import pallas as pl
from jax.experimental.pallas import tpu as pltpu
from jax.sharding import PartitionSpec as P

D = 3072
HD = 128
COLS = 128
HEADS = 7
MINE = 3
UNITS = 7
TOK = 128
FEAT = HEADS * HD
HALF = TOK // 2
PIECES = 6
STEP = D // PIECES
SCALE2 = math.log2(math.e) / math.sqrt(HD)
F32 = jnp.float32
HBM = "hbm"
BF16 = jnp.bfloat16
MIB = 1024 * 1024
COST = pl.CostEstimate(flops=1, transcendentals=0, bytes_accessed=1)
SMEM = pl.BlockSpec(memory_space=pltpu.SMEM)
VMEM = pl.BlockSpec(memory_space=pltpu.VMEM)
ANY = pl.BlockSpec(memory_space=pl.ANY)


def _place(x, y, z, c):
    return ((x * 2 + y) * 4 + z) * 2 + c


def _perm(move):
    pairs = []
    for p in range(64):
        x, y, z, c = p // 16, (p // 8) % 2, (p // 2) % 4, p % 2
        pairs.append((p, _place(*move(x, y, z, c))))
    return pairs


def _key_move(d):
    return lambda x, y, z, c: ((x + d) % 4, y, z, c) if c == 0 else (x, y, (z + d) % 4, c)


def _query_move(d):
    return lambda x, y, z, c: (x, y, (z + d) % 4, c) if c == 0 else ((x + d) % 4, y, z, c)


def _core_move(x, y, z, c):
    return (x, y, z, 1 - c)


def _y_move(x, y, z, c):
    return (x, 1 - y, z, c)


def move(array, how):
    return lax.ppermute(array, "patch", _perm(how))


def swap_heads(array):
    return lax.ppermute(array, "head", [(0, 1), (1, 0)])


def kernel_call(kernel, name, out_shape, scratch_shapes, place, scalars, *arrays, after=(), outside=(), limit=12):
    scalars = [*place, *scalars]
    begin, first, count = len(place), len(scalars) + len(outside) + len(arrays), len(after)

    def run(*refs):
        head = [[ref[0] for ref in refs[:begin]]] if begin else []
        kernel(*head, *refs[begin:first], *refs[first + count :])

    return pl.pallas_call(
        run,
        in_specs=[SMEM] * len(scalars) + [ANY] * len(outside) + [VMEM] * len(arrays) + [ANY] * count,
        out_specs=[VMEM] * len(out_shape),
        out_shape=[pltpu.VMEM(*s) if len(s) == 2 else jax.ShapeDtypeStruct(*s[:2]) for s in out_shape],
        scratch_shapes=[pltpu.VMEM(*s) if isinstance(s, tuple) else s for s in scratch_shapes],
        compiler_params=pltpu.CompilerParams(vmem_limit_bytes=limit * MIB),
        cost_estimate=COST,
        name=name,
    )(*scalars, *(pltpu.with_memory_space_constraint(a, pltpu.HBM) for a in outside), *arrays, *after)


def _turn(v, table_ref, which):
    v = v * lax.rsqrt(jnp.mean(v * v, axis=-1, keepdims=True) + 1e-06)
    lane = lax.broadcasted_iota(jnp.int32, v.shape, 1)
    other = jnp.where(lane % 2 == 0, pltpu.roll(v, HD - 1, 1), pltpu.roll(v, 1, 1))
    return v * table_ref[2 * which] + other * table_ref[2 * which + 1]


def _bring(w_ref, which, out_ref, sems):
    groups = []
    for j, i in enumerate(which):
        copies = []
        for k in range(PIECES):
            rows = pl.ds(k * STEP, STEP)
            copies.append(pltpu.make_async_copy(w_ref.at[i, rows], out_ref.at[j, rows], sems.at[j * PIECES + k]))
        for copy in copies:
            copy.start()
        groups.append(copies)
    return groups


def _stage_kernel(w_ref, image_ref, g_ref, turn_ref, out_ref, own_ref, table_ref, gain_ref, sems, more):
    copies = _bring(w_ref, (0,), out_ref, sems)[0]
    small = [pltpu.make_async_copy(g_ref, gain_ref, more.at[0]), pltpu.make_async_copy(image_ref, own_ref, more.at[1])]
    for copy in small:
        copy.start()
    small[0].wait()
    even = _lane((8, HD)) % 2 == 0
    for i in range(2):
        gain = jnp.broadcast_to(gain_ref[i : i + 1, :], (8, HD))
        swapped = jnp.where(even, pltpu.roll(gain, HD - 1, 1), pltpu.roll(gain, 1, 1))
        table_ref[2 * i] = turn_ref[0] * gain[0:1]
        table_ref[2 * i + 1] = turn_ref[1] * swapped[0:1]
    for copy in copies:
        copy.wait()
    small[1].wait()


def stage(w, image, gain, turns, after):
    scratch = [((2, HD), F32), pltpu.SemaphoreType.DMA((PIECES,)), pltpu.SemaphoreType.DMA((2,))]
    outs = [((1, D, FEAT), BF16), (image.shape, BF16), ((4, TOK, HD), F32)]
    return kernel_call(_stage_kernel, "stage", outs, scratch, [], [], turns, outside=[w, image, gain], after=after)


def _query_kernel(place, w_ref, oth_ref, own_ref, table_ref, qa_ref, qb_ref, q_ref, x_ref):
    x = jnp.concatenate([oth_ref[...], own_ref[...]], axis=0)
    x_ref[...] = x
    projected = jnp.dot(x, w_ref[0], preferred_element_type=F32)
    queries = []
    for head in range(HEADS):
        at = slice(head * HD, (head + 1) * HD)
        queries.append((_turn(projected[:, at], table_ref, 0) * SCALE2).astype(BF16))
        q_ref[head] = queries[head]
    qa_ref[MINE] = queries[MINE]
    first = place[0] == 0
    for i in range(MINE):
        low, high = queries[i], queries[i + MINE + 1]
        qa_ref[i] = jnp.where(first, low, high)
        qb_ref[i] = jnp.where(first, high, low)


def project_queries(place, *arrays):
    outs = [
        ((MINE + 1, TOK, HD), BF16),
        ((MINE, TOK, HD), BF16),
        ((HEADS, TOK, HD), BF16),
        ((TOK, D), BF16),
    ]
    return kernel_call(_query_kernel, "query_projection", outs, [], place, [], *arrays)


def _kv_kernel(place, w_ref, x_ref, table_ref, out_ref, kv_ref):
    first = pl.ds(pl.multiple_of((1 - place[1]) * HALF, HALF), HALF)
    second = pl.ds(pl.multiple_of(place[1] * HALF, HALF), HALF)
    projected = jnp.dot(x_ref[...], w_ref[1], preferred_element_type=F32)
    for head in range(HEADS):
        at = slice(head * HD, (head + 1) * HD)
        k = _turn(projected[:, at], table_ref, 1).astype(BF16)
        out_ref[0, first, at] = k[:HALF]
        out_ref[0, second, at] = k[HALF:]
        kv_ref[0, :, at] = k
    v = jnp.dot(x_ref[...], w_ref[2], preferred_element_type=F32).astype(BF16)
    out_ref[1, first, :] = v[:HALF]
    out_ref[1, second, :] = v[HALF:]
    kv_ref[1] = v


def project_keys(place, *arrays, after):
    outs = [((2, TOK, FEAT), BF16, HBM), ((2, TOK, FEAT), BF16)]
    return kernel_call(_kv_kernel, "key_value_projection", outs, [], place, [], *arrays, after=after)


def _home_kernel(count, text, q_ref, kv_ref, home_ref, stat_ref, s_ref):
    slots = text.shape[1]

    def score(head):
        at = slice(head * HD, (head + 1) * HD)
        s_ref[head, :, slots:] = _scores(q_ref[head], kv_ref[0, :, at])
        s = _scores(q_ref[head], text[0, :, at])
        s_ref[head, :, :slots] = jnp.where(_lane(s.shape) < count[0], s, -jnp.inf)

    stat = jnp.zeros((TOK, HD), F32)
    score(0)
    for head in range(HEADS):
        if head + 1 < HEADS:
            score(head + 1)
        at = slice(head * HD, (head + 1) * HD)
        peak, out = _fold(s_ref[head], None, jnp.concatenate([text[1, :, at], kv_ref[1, :, at]], axis=0))
        total = out[:, HD:]
        home_ref[head] = (out[:, :HD] / total).astype(BF16)
        stat = jnp.where(_lane(stat.shape) == head, peak + jnp.log2(total), stat)
    stat_ref[...] = stat


def attend_home(count, text_kv, *arrays, after):
    outs = [((HEADS, TOK, HD), BF16), ((TOK, HD), F32)]
    scratch = [((HEADS, TOK, text_kv.shape[1] + TOK), F32)]
    return kernel_call(_home_kernel, "home_attention", outs, scratch, [], [count], text_kv, *arrays, after=after)


def _join_kernel(a_ref, b_ref, out_ref):
    out_ref[: MINE + 1] = a_ref[...]
    out_ref[MINE + 1 :] = b_ref[...]


def _gate_kernel(a_ref, *refs):
    del a_ref, refs


def gate(array, after):
    return pl.pallas_call(
        _gate_kernel,
        in_specs=[ANY] * (1 + len(after)),
        out_specs=ANY,
        out_shape=pltpu.VMEM(array.shape, array.dtype),
        input_output_aliases={0: 0},
        compiler_params=pltpu.CompilerParams(vmem_limit_bytes=MIB),
        cost_estimate=COST,
        name="gate",
    )(pltpu.with_memory_space_constraint(array, pltpu.VMEM), *after)


def join_units(a, b, after):
    outs = [((UNITS, TOK, HD), BF16)]
    return kernel_call(_join_kernel, "join_units", outs, [], [], [], a, b, after=after)[0]


def _scores(q, k):
    return lax.dot_general(q, k, (((1,), (1,)), ((), ())), preferred_element_type=F32)


def _fold(s, peak, values):
    top = s[:, :HD]
    for t in range(1, s.shape[1] // HD):
        top = jnp.maximum(top, s[:, t * HD : (t + 1) * HD])
    top = jnp.max(top, axis=1, keepdims=True)
    if peak is not None:
        top = jnp.maximum(top, peak)
    raw = jnp.exp2(s - top).astype(BF16)
    wide = jnp.concatenate([values, jnp.ones((values.shape[0], HD), BF16)], axis=1)
    return top, jnp.dot(raw, wide, preferred_element_type=F32)


def _lane(shape):
    return lax.broadcasted_iota(jnp.int32, shape, 1)


def _put(stat, u, peak, total):
    lane = _lane(stat.shape)
    return jnp.where(lane == u, peak, jnp.where(lane == u + 16, total, stat))


def _cols(index):
    return pl.ds(pl.multiple_of(index * HD, HD), HD)


def _slot_of(u, c):
    if u == MINE:
        return MINE * (1 - c)
    return (u if u < MINE else u - MINE - 1) + c


ORDER = ((1, 2, 3, 0), (0, 1, 2, 3))
OWN = (slice(3 * HALF, 4 * HALF), slice(0, HALF))
ROWS = (((1, 0), (2, 0), (3, 0)), ((0, 0), (0, 1), (1, 1), (2, 1), (3, 1)))


def _gather(refs, u, rows):
    return jnp.concatenate([refs[i][u, g * HALF : (g + 1) * HALF] for i, g in rows], axis=0)


def _near_kernel(place, *refs):
    queries, keys = refs[:4], refs[4:8]
    acc_ref, stat_ref, s_ref = refs[8:]
    c = place[0]
    steps = [(u, g) for u in range(UNITS) for g in range(2)]

    def score(i):
        u, g = steps[i]
        q = _gather(queries, u, [(r, g) for r in ORDER[g]])
        for b, k in enumerate(keys):
            s = _scores(q, k[0, :, _cols(_slot_of(u, c))])
            s_ref[i % 2, :, b * 2 * TOK : (b + 1) * 2 * TOK] = s
        patch = slice(0, TOK) if u <= MINE else slice(TOK, 2 * TOK)
        s_ref[i % 2, OWN[g], patch] = jnp.full((HALF, TOK), -jnp.inf, F32)

    stats = [jnp.zeros((4 * HALF, HD), F32)] * 2
    score(0)
    for i, (u, g) in enumerate(steps):
        if i + 1 < len(steps):
            score(i + 1)
        values = jnp.concatenate([k[1, :, _cols(_slot_of(u, c))] for k in keys], axis=0)
        peak, out = _fold(s_ref[i % 2], None, values)
        acc_ref[u, g * 4 * HALF : (g + 1) * 4 * HALF] = out[:, :HD]
        stats[g] = _put(stats[g], u, peak, out[:, HD:])
    stat_ref[: 4 * HALF] = stats[0]
    stat_ref[4 * HALF :] = stats[1]


def attend_near(place, queries, pairs, after):
    outs = [((UNITS, 4 * TOK, HD), F32), ((4 * TOK, HD), F32)]
    scratch = [((2, 4 * HALF, 8 * TOK), F32)]
    return kernel_call(_near_kernel, "near_attention", outs, scratch, place, [], *queries, *pairs, after=after)


def _far_kernel(g, place, *refs):
    queries, (acc_in, stat_in), keys = refs[:4], refs[4:6], refs[6:10]
    outs, s_ref = refs[10:-1], refs[-1]
    c = place[0]
    count = len(ROWS[g]) * HALF
    rows = slice(0, count) if g == 0 else slice(4 * TOK - count, 4 * TOK)

    def score(u):
        q = _gather(queries, u, ROWS[g])
        for b, k in enumerate(keys):
            s = _scores(q, k[0, :, _cols(_slot_of(u, c))])
            s_ref[u % 2, :, b * 2 * TOK : (b + 1) * 2 * TOK] = s

    mark = jnp.zeros((count, HD), F32)
    score(0)
    for u in range(UNITS):
        if u + 1 < UNITS:
            score(u + 1)
        before = stat_in[rows, u : u + 1]
        values = jnp.concatenate([k[1, :, _cols(_slot_of(u, c))] for k in keys], axis=0)
        peak, out = _fold(s_ref[u % 2], before, values)
        factor = jnp.exp2(before - peak)
        total = stat_in[rows, u + 16 : u + 17] * factor + out[:, HD:]
        out = ((acc_in[u, rows] * factor + out[:, :HD]) / total).astype(BF16)
        level = peak + jnp.log2(total)
        mark = jnp.where(_lane(level.shape) % 16 == u, level, mark)
        _deal(outs, u, out)
    _deal(outs, UNITS, _spread(mark))


def _deal(outs, u, rows):
    at = 0
    for o in outs:
        o[u] = rows[at : at + o.shape[1]]
        at += o.shape[1]


def attend_far(g, place, queries, acc, stat, pairs, after):
    outs = [((UNITS + 1, HALF, HD), BF16)] * 3
    if g == 1:
        outs = [((UNITS + 1, TOK, HD), BF16)] + outs
    scratch = [((2, len(ROWS[g]) * HALF, 8 * TOK), F32)]
    kernel = functools.partial(_far_kernel, g)
    arrays = (*queries, acc, stat, *pairs)
    return kernel_call(kernel, f"far_attention_{g}", outs, scratch, place, [], *arrays, after=after)


def _spread(level):
    high = level.astype(BF16).astype(F32)
    middle = (level - high).astype(BF16).astype(F32)
    lane = _lane(level.shape)
    low = level - high - middle
    return jnp.where(lane < 16, high, jnp.where(lane < 32, middle, low)).astype(BF16)


def _collect(mark):
    mark = mark.astype(F32)
    return mark + pltpu.roll(mark, HD - 16, 1) + pltpu.roll(mark, HD - 32, 1)


def _merge_kernel(g, p0, p1, p2, p3, mine_ref, stat_ref, sib_ref):
    parts = (p0.at[:, g * HALF : (g + 1) * HALF], p1, p2, p3)
    levels = [_collect(p[UNITS]) for p in parts]
    top = functools.reduce(jnp.maximum, levels)
    weights = [jnp.exp2(v - top) for v in levels]
    total = functools.reduce(jnp.add, weights)
    weights = [w / total for w in weights]
    for u in range(UNITS):
        out = None
        for p, w in zip(parts, weights, strict=True):
            term = p[u].astype(F32) * w[:, u : u + 1]
            out = term if out is None else out + term
        if u <= MINE:
            mine_ref[u] = out.astype(BF16)
        else:
            sib_ref[u - MINE - 1] = out.astype(BF16)
    level = top + jnp.log2(total)
    stat_ref[...] = level
    lane = _lane(level.shape)
    level = jnp.where(lane < 16, level, 0.0)
    sib_ref[MINE] = _spread(level + pltpu.roll(level, 16, 1) + pltpu.roll(level, 32, 1))


def merge(g, parts):
    outs = [((MINE + 1, HALF, HD), BF16), ((HALF, HD), F32), ((MINE + 1, HALF, HD), BF16)]
    return kernel_call(functools.partial(_merge_kernel, g), "merge_parts", outs, [], [], [], *parts)


def _out_kernel(g, place, mine_ref, stat_ref, got_ref, home_ref, level_ref, w_ref, *rest):
    *other, out_ref = rest
    rows = slice(g * HALF, (g + 1) * HALF)
    first = place[0] == 0
    mine = stat_ref[...]
    got = _collect(got_ref[MINE])
    attended = []
    for head in range(HEADS):
        slot = head % (MINE + 1)
        a, la = mine_ref[slot], mine[:, slot : slot + 1]
        if head != MINE:
            low = head < MINE
            b, lb = got_ref[slot], got[:, slot + MINE + 1 : slot + MINE + 2]
            a, b = (a, b) if low else (b, a)
            la, lb = (la, lb) if low else (lb, la)
            a, la = jnp.where(first, a, b), jnp.where(first, la, lb)
        h, lh = home_ref[head, rows], level_ref[rows, head : head + 1]
        top = jnp.maximum(la, lh)
        wa, wh = jnp.exp2(la - top), jnp.exp2(lh - top)
        total = wa + wh
        out = a.astype(F32) * (wa / total) + h.astype(F32) * (wh / total)
        attended.append(out.astype(BF16))
    out = jnp.dot(jnp.concatenate(attended, axis=1), w_ref[...], preferred_element_type=F32)
    for ref in other:
        out = out + ref[...].astype(F32)
    out_ref[...] = out.astype(BF16)


def project_out(g, place, *arrays, after):
    outs = [((HALF, D), BF16, HBM)]
    kernel = functools.partial(_out_kernel, g)
    return kernel_call(kernel, "output_projection", outs, [], place, [], *arrays, after=after)[0]


def _bands():
    first = HD // 8
    band = (HD - first) // 2
    omega = np.repeat(10000.0 ** (-2.0 * np.arange(band // 2) / band), 2)
    along_rows = np.zeros((HD,))
    along_cols = np.zeros((HD,))
    along_rows[first : first + band] = omega
    along_cols[first + band :] = omega
    sign = np.where(np.arange(HD) % 2 == 0, -1.0, 1.0)
    return (v.astype(np.float32) for v in (along_rows, along_cols, sign))


def body(image, w_qkv, qk_gain, stale_kv, text_kv, text_count, row_offset, w_out):
    core = lax.axis_index("patch") % 2
    group = lax.axis_index("head")
    place = [core.astype(jnp.int32).reshape(1), group.astype(jnp.int32).reshape(1)]
    other_image = swap_heads(image)

    wide = (2, TOK, (MINE + 1) * HD)
    given = lax.dynamic_slice(stale_kv, (0, 0, (1 - core) * MINE * HD), wide)
    kept = lax.dynamic_slice(stale_kv, (0, 0, core * MINE * HD), wide)
    pair = jnp.concatenate([kept, move(given, _core_move)], axis=1)
    far_pair = move(pair, _y_move)
    near = [pair] + [move(pair, _key_move(d)) for d in (1, 3, 2)]

    within = jnp.arange(TOK, dtype=jnp.int32)
    within = jnp.where(within < HALF, within + (1 - group) * HALF, within - (1 - group) * HALF)
    rows = (row_offset[0] + within // COLS).astype(F32)[:, None]
    cols = (within % COLS).astype(F32)[:, None]
    along_rows, along_cols, sign = _bands()
    angles = rows * along_rows + cols * along_cols
    turns = jnp.stack([jnp.cos(angles), jnp.sin(angles) * sign])

    w = jnp.transpose(w_qkv, (1, 0, 2))
    staged, own_image, table = stage(w, image, qk_gain, turns, [pair])
    q_mine, q_given, q_own, x = project_queries(place, staged, other_image, own_image, table)
    units = join_units(q_mine, move(q_given, _core_move), near[1:3])
    queries = [units] + [move(units, _query_move(d)) for d in (1, 3, 2)]
    far_two = move(near[3], _y_move)
    fresh_kv, kv = project_keys(place, w, x, table, after=[units, near[3]])
    far_pair = gate(far_pair, queries[1:4] + [kv])
    far = [far_pair] + [move(far_pair, _key_move(d)) for d in (1, 3)] + [far_two]
    home, level = attend_home(text_count, text_kv, q_own, kv, after=[far_pair])
    acc, stat = attend_near(place, queries, near, [home])

    first = attend_far(0, place, queries, acc, stat, far, [])
    own, *second = attend_far(1, place, queries, acc, stat, far, [])
    back = [[own] + [move(p, _query_move(d)) for p, d in zip(parts, (3, 1, 2))] for parts in (first, second)]
    merged = [merge(g, back[g]) for g in (0, 1)]
    got = [move(merged[g][2], _core_move) for g in (0, 1)]
    sent = project_out(0, place, *merged[0][:2], got[0], home, level, w_out, after=[])
    mixed = project_out(1, place, *merged[1][:2], got[1], home, level, w_out, swap_heads(sent), after=[])
    return (mixed, fresh_kv)


def solution(mesh):
    placed = (
        P(("patch", "head"), None),
        P(None, None, "head"),
        P(),
        P(None, "patch", "head"),
        P(None, None, "head"),
        P(),
        P("patch"),
        P("head", None),
    )
    return jax.shard_map(
        body,
        mesh=mesh,
        in_specs=placed,
        out_specs=(P(("patch", "head"), None), P(None, "patch", "head")),
        check_vma=False,
    )
```

```python
import functools
import math

import jax
import jax.numpy as jnp
import numpy as np
from jax import lax
from jax.experimental import pallas as pl
from jax.experimental.pallas import tpu as pltpu
from jax.sharding import PartitionSpec as P

D = 3072
HD = 128
COLS = 128
HEADS = 7
MINE = 3
UNITS = 7
TOK = 128
FEAT = HEADS * HD
HALF = TOK // 2
PIECES = 6
STEP = D // PIECES
SCALE2 = math.log2(math.e) / math.sqrt(HD)
F32 = jnp.float32
HBM = "hbm"
BF16 = jnp.bfloat16
MIB = 1024 * 1024
COST = pl.CostEstimate(flops=1, transcendentals=0, bytes_accessed=1)
SMEM = pl.BlockSpec(memory_space=pltpu.SMEM)
VMEM = pl.BlockSpec(memory_space=pltpu.VMEM)
ANY = pl.BlockSpec(memory_space=pl.ANY)


def _place(x, y, z, c):
    return ((x * 2 + y) * 4 + z) * 2 + c


def _perm(move):
    pairs = []
    for p in range(64):
        x, y, z, c = p // 16, (p // 8) % 2, (p // 2) % 4, p % 2
        pairs.append((p, _place(*move(x, y, z, c))))
    return pairs


def _key_move(d):
    return lambda x, y, z, c: ((x + d) % 4, y, z, c) if c == 0 else (x, y, (z + d) % 4, c)


def _query_move(d):
    return lambda x, y, z, c: (x, y, (z + d) % 4, c) if c == 0 else ((x + d) % 4, y, z, c)


def _core_move(x, y, z, c):
    return (x, y, z, 1 - c)


def _y_move(x, y, z, c):
    return (x, 1 - y, z, c)


def move(array, how):
    return lax.ppermute(array, "patch", _perm(how))


def swap_heads(array):
    return lax.ppermute(array, "head", [(0, 1), (1, 0)])


def kernel_call(kernel, name, out_shape, scratch_shapes, place, scalars, *arrays, after=(), outside=(), limit=12):
    scalars = [*place, *scalars]
    begin, first, count = len(place), len(scalars) + len(outside) + len(arrays), len(after)

    def run(*refs):
        head = [[ref[0] for ref in refs[:begin]]] if begin else []
        kernel(*head, *refs[begin:first], *refs[first + count :])

    return pl.pallas_call(
        run,
        in_specs=[SMEM] * len(scalars) + [ANY] * len(outside) + [VMEM] * len(arrays) + [ANY] * count,
        out_specs=[VMEM] * len(out_shape),
        out_shape=[pltpu.VMEM(*s) if len(s) == 2 else jax.ShapeDtypeStruct(*s[:2]) for s in out_shape],
        scratch_shapes=[pltpu.VMEM(*s) if isinstance(s, tuple) else s for s in scratch_shapes],
        compiler_params=pltpu.CompilerParams(vmem_limit_bytes=limit * MIB),
        cost_estimate=COST,
        name=name,
    )(*scalars, *(pltpu.with_memory_space_constraint(a, pltpu.HBM) for a in outside), *arrays, *after)


def _turn(v, table_ref, which):
    v = v * lax.rsqrt(jnp.mean(v * v, axis=-1, keepdims=True) + 1e-06)
    lane = lax.broadcasted_iota(jnp.int32, v.shape, 1)
    other = jnp.where(lane % 2 == 0, pltpu.roll(v, HD - 1, 1), pltpu.roll(v, 1, 1))
    return v * table_ref[2 * which] + other * table_ref[2 * which + 1]


def _bring(w_ref, which, out_ref, sems):
    groups = []
    for j, i in enumerate(which):
        copies = []
        for k in range(PIECES):
            rows = pl.ds(k * STEP, STEP)
            copies.append(pltpu.make_async_copy(w_ref.at[i, rows], out_ref.at[j, rows], sems.at[j * PIECES + k]))
        for copy in copies:
            copy.start()
        groups.append(copies)
    return groups


def _stage_kernel(w_ref, image_ref, g_ref, turn_ref, out_ref, own_ref, table_ref, gain_ref, sems, more):
    copies = _bring(w_ref, (0,), out_ref, sems)[0]
    small = [pltpu.make_async_copy(g_ref, gain_ref, more.at[0]), pltpu.make_async_copy(image_ref, own_ref, more.at[1])]
    for copy in small:
        copy.start()
    small[0].wait()
    even = _lane((8, HD)) % 2 == 0
    for i in range(2):
        gain = jnp.broadcast_to(gain_ref[i : i + 1, :], (8, HD))
        swapped = jnp.where(even, pltpu.roll(gain, HD - 1, 1), pltpu.roll(gain, 1, 1))
        table_ref[2 * i] = turn_ref[0] * gain[0:1]
        table_ref[2 * i + 1] = turn_ref[1] * swapped[0:1]
    for copy in copies:
        copy.wait()
    small[1].wait()


def stage(w, image, gain, turns, after):
    scratch = [((2, HD), F32), pltpu.SemaphoreType.DMA((PIECES,)), pltpu.SemaphoreType.DMA((2,))]
    outs = [((1, D, FEAT), BF16), (image.shape, BF16), ((4, TOK, HD), F32)]
    return kernel_call(_stage_kernel, "stage", outs, scratch, [], [], turns, outside=[w, image, gain], after=after)


def _query_kernel(place, w_ref, oth_ref, own_ref, table_ref, qa_ref, qb_ref, q_ref, x_ref):
    x = jnp.concatenate([oth_ref[...], own_ref[...]], axis=0)
    x_ref[...] = x
    projected = jnp.dot(x, w_ref[0], preferred_element_type=F32)
    queries = []
    for head in range(HEADS):
        at = slice(head * HD, (head + 1) * HD)
        queries.append((_turn(projected[:, at], table_ref, 0) * SCALE2).astype(BF16))
        q_ref[head] = queries[head]
    qa_ref[MINE] = queries[MINE]
    first = place[0] == 0
    for i in range(MINE):
        low, high = queries[i], queries[i + MINE + 1]
        qa_ref[i] = jnp.where(first, low, high)
        qb_ref[i] = jnp.where(first, high, low)


def project_queries(place, *arrays):
    outs = [
        ((MINE + 1, TOK, HD), BF16),
        ((MINE, TOK, HD), BF16),
        ((HEADS, TOK, HD), BF16),
        ((TOK, D), BF16),
    ]
    return kernel_call(_query_kernel, "query_projection", outs, [], place, [], *arrays)


def _kv_kernel(place, w_ref, x_ref, table_ref, out_ref, kv_ref):
    first = pl.ds(pl.multiple_of((1 - place[1]) * HALF, HALF), HALF)
    second = pl.ds(pl.multiple_of(place[1] * HALF, HALF), HALF)
    projected = jnp.dot(x_ref[...], w_ref[1], preferred_element_type=F32)
    for head in range(HEADS):
        at = slice(head * HD, (head + 1) * HD)
        k = _turn(projected[:, at], table_ref, 1).astype(BF16)
        out_ref[0, first, at] = k[:HALF]
        out_ref[0, second, at] = k[HALF:]
        kv_ref[0, :, at] = k
    v = jnp.dot(x_ref[...], w_ref[2], preferred_element_type=F32).astype(BF16)
    out_ref[1, first, :] = v[:HALF]
    out_ref[1, second, :] = v[HALF:]
    kv_ref[1] = v


def project_keys(place, *arrays, after):
    outs = [((2, TOK, FEAT), BF16, HBM), ((2, TOK, FEAT), BF16)]
    return kernel_call(_kv_kernel, "key_value_projection", outs, [], place, [], *arrays, after=after)


def _home_kernel(count, text, q_ref, kv_ref, home_ref, stat_ref, s_ref):
    slots = text.shape[1]

    def score(head):
        at = slice(head * HD, (head + 1) * HD)
        s_ref[head, :, slots:] = _scores(q_ref[head], kv_ref[0, :, at])
        s = _scores(q_ref[head], text[0, :, at])
        s_ref[head, :, :slots] = jnp.where(_lane(s.shape) < count[0], s, -jnp.inf)

    stat = jnp.zeros((TOK, HD), F32)
    score(0)
    for head in range(HEADS):
        if head + 1 < HEADS:
            score(head + 1)
        at = slice(head * HD, (head + 1) * HD)
        peak, out = _fold(s_ref[head], None, jnp.concatenate([text[1, :, at], kv_ref[1, :, at]], axis=0))
        total = out[:, HD:]
        home_ref[head] = (out[:, :HD] / total).astype(BF16)
        stat = jnp.where(_lane(stat.shape) == head, peak + jnp.log2(total), stat)
    stat_ref[...] = stat


def attend_home(count, text_kv, *arrays, after):
    outs = [((HEADS, TOK, HD), BF16), ((TOK, HD), F32)]
    scratch = [((HEADS, TOK, text_kv.shape[1] + TOK), F32)]
    return kernel_call(_home_kernel, "home_attention", outs, scratch, [], [count], text_kv, *arrays, after=after)


def _join_kernel(a_ref, b_ref, out_ref):
    out_ref[: MINE + 1] = a_ref[...]
    out_ref[MINE + 1 :] = b_ref[...]


def _gate_kernel(a_ref, *refs):
    del a_ref, refs


def gate(array, after):
    return pl.pallas_call(
        _gate_kernel,
        in_specs=[ANY] * (1 + len(after)),
        out_specs=ANY,
        out_shape=pltpu.VMEM(array.shape, array.dtype),
        input_output_aliases={0: 0},
        compiler_params=pltpu.CompilerParams(vmem_limit_bytes=MIB),
        cost_estimate=COST,
        name="gate",
    )(pltpu.with_memory_space_constraint(array, pltpu.VMEM), *after)


def join_units(a, b, after):
    outs = [((UNITS, TOK, HD), BF16)]
    return kernel_call(_join_kernel, "join_units", outs, [], [], [], a, b, after=after)[0]


def _scores(q, k):
    return lax.dot_general(q, k, (((1,), (1,)), ((), ())), preferred_element_type=F32)


def _fold(s, peak, values):
    top = s[:, :HD]
    for t in range(1, s.shape[1] // HD):
        top = jnp.maximum(top, s[:, t * HD : (t + 1) * HD])
    top = jnp.max(top, axis=1, keepdims=True)
    if peak is not None:
        top = jnp.maximum(top, peak)
    raw = jnp.exp2(s - top).astype(BF16)
    wide = jnp.concatenate([values, jnp.ones((values.shape[0], HD), BF16)], axis=1)
    return top, jnp.dot(raw, wide, preferred_element_type=F32)


def _lane(shape):
    return lax.broadcasted_iota(jnp.int32, shape, 1)


def _put(stat, u, peak, total):
    lane = _lane(stat.shape)
    return jnp.where(lane == u, peak, jnp.where(lane == u + 16, total, stat))


def _cols(index):
    return pl.ds(pl.multiple_of(index * HD, HD), HD)


def _slot_of(u, c):
    if u == MINE:
        return MINE * (1 - c)
    return (u if u < MINE else u - MINE - 1) + c


ORDER = ((1, 2, 3, 0), (0, 1, 2, 3))
OWN = (slice(3 * HALF, 4 * HALF), slice(0, HALF))
ROWS = (((1, 0), (2, 0), (3, 0)), ((0, 0), (0, 1), (1, 1), (2, 1), (3, 1)))


def _gather(refs, u, rows):
    return jnp.concatenate([refs[i][u, g * HALF : (g + 1) * HALF] for i, g in rows], axis=0)


def _near_kernel(place, *refs):
    queries, keys = refs[:4], refs[4:8]
    acc_ref, stat_ref, s_ref = refs[8:]
    c = place[0]
    steps = [(u, g) for u in range(UNITS) for g in range(2)]

    def score(i):
        u, g = steps[i]
        q = _gather(queries, u, [(r, g) for r in ORDER[g]])
        for b, k in enumerate(keys):
            s = _scores(q, k[0, :, _cols(_slot_of(u, c))])
            s_ref[i % 2, :, b * 2 * TOK : (b + 1) * 2 * TOK] = s
        patch = slice(0, TOK) if u <= MINE else slice(TOK, 2 * TOK)
        s_ref[i % 2, OWN[g], patch] = jnp.full((HALF, TOK), -jnp.inf, F32)

    stats = [jnp.zeros((4 * HALF, HD), F32)] * 2
    score(0)
    for i, (u, g) in enumerate(steps):
        if i + 1 < len(steps):
            score(i + 1)
        values = jnp.concatenate([k[1, :, _cols(_slot_of(u, c))] for k in keys], axis=0)
        peak, out = _fold(s_ref[i % 2], None, values)
        acc_ref[u, g * 4 * HALF : (g + 1) * 4 * HALF] = out[:, :HD]
        stats[g] = _put(stats[g], u, peak, out[:, HD:])
    stat_ref[: 4 * HALF] = stats[0]
    stat_ref[4 * HALF :] = stats[1]


def attend_near(place, queries, pairs, after):
    outs = [((UNITS, 4 * TOK, HD), F32), ((4 * TOK, HD), F32)]
    scratch = [((2, 4 * HALF, 8 * TOK), F32)]
    return kernel_call(_near_kernel, "near_attention", outs, scratch, place, [], *queries, *pairs, after=after)


def _far_kernel(g, place, *refs):
    queries, (acc_in, stat_in), keys = refs[:4], refs[4:6], refs[6:10]
    outs, s_ref = refs[10:-1], refs[-1]
    c = place[0]
    count = len(ROWS[g]) * HALF
    rows = slice(0, count) if g == 0 else slice(4 * TOK - count, 4 * TOK)

    def score(u):
        q = _gather(queries, u, ROWS[g])
        for b, k in enumerate(keys):
            s = _scores(q, k[0, :, _cols(_slot_of(u, c))])
            s_ref[u % 2, :, b * 2 * TOK : (b + 1) * 2 * TOK] = s

    mark = jnp.zeros((count, HD), F32)
    score(0)
    for u in range(UNITS):
        if u + 1 < UNITS:
            score(u + 1)
        before = stat_in[rows, u : u + 1]
        values = jnp.concatenate([k[1, :, _cols(_slot_of(u, c))] for k in keys], axis=0)
        peak, out = _fold(s_ref[u % 2], before, values)
        factor = jnp.exp2(before - peak)
        total = stat_in[rows, u + 16 : u + 17] * factor + out[:, HD:]
        out = ((acc_in[u, rows] * factor + out[:, :HD]) / total).astype(BF16)
        level = peak + jnp.log2(total)
        mark = jnp.where(_lane(level.shape) % 16 == u, level, mark)
        _deal(outs, u, out)
    _deal(outs, UNITS, _spread(mark))


def _deal(outs, u, rows):
    at = 0
    for o in outs:
        o[u] = rows[at : at + o.shape[1]]
        at += o.shape[1]


def attend_far(g, place, queries, acc, stat, pairs, after):
    outs = [((UNITS + 1, HALF, HD), BF16)] * 3
    if g == 1:
        outs = [((UNITS + 1, TOK, HD), BF16)] + outs
    scratch = [((2, len(ROWS[g]) * HALF, 8 * TOK), F32)]
    kernel = functools.partial(_far_kernel, g)
    arrays = (*queries, acc, stat, *pairs)
    return kernel_call(kernel, f"far_attention_{g}", outs, scratch, place, [], *arrays, after=after)


def _spread(level):
    high = level.astype(BF16).astype(F32)
    middle = (level - high).astype(BF16).astype(F32)
    lane = _lane(level.shape)
    low = level - high - middle
    return jnp.where(lane < 16, high, jnp.where(lane < 32, middle, low)).astype(BF16)


def _collect(mark):
    mark = mark.astype(F32)
    return mark + pltpu.roll(mark, HD - 16, 1) + pltpu.roll(mark, HD - 32, 1)


def _merge_kernel(g, p0, p1, p2, p3, mine_ref, stat_ref, sib_ref):
    parts = (p0.at[:, g * HALF : (g + 1) * HALF], p1, p2, p3)
    levels = [_collect(p[UNITS]) for p in parts]
    top = functools.reduce(jnp.maximum, levels)
    weights = [jnp.exp2(v - top) for v in levels]
    total = functools.reduce(jnp.add, weights)
    weights = [w / total for w in weights]
    for u in range(UNITS):
        out = None
        for p, w in zip(parts, weights, strict=True):
            term = p[u].astype(F32) * w[:, u : u + 1]
            out = term if out is None else out + term
        if u <= MINE:
            mine_ref[u] = out.astype(BF16)
        else:
            sib_ref[u - MINE - 1] = out.astype(BF16)
    level = top + jnp.log2(total)
    stat_ref[...] = level
    lane = _lane(level.shape)
    level = jnp.where(lane < 16, level, 0.0)
    sib_ref[MINE] = _spread(level + pltpu.roll(level, 16, 1) + pltpu.roll(level, 32, 1))


def merge(g, parts):
    outs = [((MINE + 1, HALF, HD), BF16), ((HALF, HD), F32), ((MINE + 1, HALF, HD), BF16)]
    return kernel_call(functools.partial(_merge_kernel, g), "merge_parts", outs, [], [], [], *parts)


def _blend(a, la, h, lh):
    top = jnp.maximum(la, lh)
    wa, wh = jnp.exp2(la - top), jnp.exp2(lh - top)
    total = wa + wh
    return (a.astype(F32) * (wa / total) + h.astype(F32) * (wh / total)).astype(BF16)


def _rows(head):
    return pl.ds(pl.multiple_of(head * HD, HD), HD)


def _mine_kernel(g, place, mine_ref, stat_ref, home_ref, level_ref, w_ref, out_ref):
    rows = slice(g * HALF, (g + 1) * HALF)
    c = place[0]
    low, mine, level = c == 0, stat_ref[...], level_ref[rows]
    attended, weights = [], []
    for slot in range(MINE + 1):
        high = slot if slot == MINE else slot + MINE + 1
        head = slot + (high - slot) * c
        lh = jnp.where(low, level[:, slot : slot + 1], level[:, high : high + 1])
        attended.append(_blend(mine_ref[slot], mine[:, slot : slot + 1], home_ref[head, rows], lh))
        weights.append(w_ref[_rows(head), :])
    attended, weights = jnp.concatenate(attended, axis=1), jnp.concatenate(weights, axis=0)
    out_ref[...] = jnp.dot(attended, weights, preferred_element_type=F32)


def _got_kernel(g, place, part_ref, got_ref, home_ref, level_ref, w_ref, *rest):
    *other, out_ref = rest
    rows = slice(g * HALF, (g + 1) * HALF)
    c = place[0]
    low, level = c == 0, level_ref[rows]
    got = _collect(got_ref[MINE])
    attended, weights = [], []
    for slot in range(MINE):
        high = slot + MINE + 1
        head = high - (high - slot) * c
        lh = jnp.where(low, level[:, high : high + 1], level[:, slot : slot + 1])
        attended.append(_blend(got_ref[slot], got[:, high : high + 1], home_ref[head, rows], lh))
        weights.append(w_ref[_rows(head), :])
    attended, weights = jnp.concatenate(attended, axis=1), jnp.concatenate(weights, axis=0)
    out = part_ref[...] + jnp.dot(attended, weights, preferred_element_type=F32)
    for ref in other:
        out = out + ref[...].astype(F32)
    out_ref[...] = out.astype(BF16)


def project_out(g, place, mine, stat, got, home, level, w_out, *other):
    outs = [((HALF, D), F32)]
    arrays = (mine, stat, home, level, w_out)
    kernel = functools.partial(_mine_kernel, g)
    part = kernel_call(kernel, "output_projection_mine", outs, [], place, [], *arrays)[0]
    outs = [((HALF, D), BF16, HBM)]
    arrays = (part, got, home, level, w_out, *other)
    kernel = functools.partial(_got_kernel, g)
    return kernel_call(kernel, "output_projection_got", outs, [], place, [], *arrays)[0]


def _bands():
    first = HD // 8
    band = (HD - first) // 2
    omega = np.repeat(10000.0 ** (-2.0 * np.arange(band // 2) / band), 2)
    along_rows = np.zeros((HD,))
    along_cols = np.zeros((HD,))
    along_rows[first : first + band] = omega
    along_cols[first + band :] = omega
    sign = np.where(np.arange(HD) % 2 == 0, -1.0, 1.0)
    return (v.astype(np.float32) for v in (along_rows, along_cols, sign))


def body(image, w_qkv, qk_gain, stale_kv, text_kv, text_count, row_offset, w_out):
    core = lax.axis_index("patch") % 2
    group = lax.axis_index("head")
    place = [core.astype(jnp.int32).reshape(1), group.astype(jnp.int32).reshape(1)]
    other_image = swap_heads(image)

    wide = (2, TOK, (MINE + 1) * HD)
    given = lax.dynamic_slice(stale_kv, (0, 0, (1 - core) * MINE * HD), wide)
    kept = lax.dynamic_slice(stale_kv, (0, 0, core * MINE * HD), wide)
    pair = jnp.concatenate([kept, move(given, _core_move)], axis=1)
    far_pair = move(pair, _y_move)
    near = [pair] + [move(pair, _key_move(d)) for d in (1, 3, 2)]

    within = jnp.arange(TOK, dtype=jnp.int32)
    within = jnp.where(within < HALF, within + (1 - group) * HALF, within - (1 - group) * HALF)
    rows = (row_offset[0] + within // COLS).astype(F32)[:, None]
    cols = (within % COLS).astype(F32)[:, None]
    along_rows, along_cols, sign = _bands()
    angles = rows * along_rows + cols * along_cols
    turns = jnp.stack([jnp.cos(angles), jnp.sin(angles) * sign])

    w = jnp.transpose(w_qkv, (1, 0, 2))
    staged, own_image, table = stage(w, image, qk_gain, turns, [pair])
    q_mine, q_given, q_own, x = project_queries(place, staged, other_image, own_image, table)
    units = join_units(q_mine, move(q_given, _core_move), near[1:3])
    queries = [units] + [move(units, _query_move(d)) for d in (1, 3, 2)]
    far_two = move(near[3], _y_move)
    fresh_kv, kv = project_keys(place, w, x, table, after=[units, near[3]])
    far_pair = gate(far_pair, queries[1:4] + [kv])
    far = [far_pair] + [move(far_pair, _key_move(d)) for d in (1, 3)] + [far_two]
    home, level = attend_home(text_count, text_kv, q_own, kv, after=[far_pair])
    acc, stat = attend_near(place, queries, near, [home])

    first = attend_far(0, place, queries, acc, stat, far, [])
    own, *second = attend_far(1, place, queries, acc, stat, far, [])
    back = [[own] + [move(p, _query_move(d)) for p, d in zip(parts, (3, 1, 2))] for parts in (first, second)]
    merged = [merge(g, back[g]) for g in (0, 1)]
    got = [move(merged[g][2], _core_move) for g in (0, 1)]
    sent = project_out(0, place, *merged[0][:2], got[0], home, level, w_out)
    mixed = project_out(1, place, *merged[1][:2], got[1], home, level, w_out, swap_heads(sent))
    return (mixed, fresh_kv)


def solution(mesh):
    placed = (
        P(("patch", "head"), None),
        P(None, None, "head"),
        P(),
        P(None, "patch", "head"),
        P(None, None, "head"),
        P(),
        P("patch"),
        P("head", None),
    )
    return jax.shard_map(
        body,
        mesh=mesh,
        in_specs=placed,
        out_specs=(P(("patch", "head"), None), P(None, "patch", "head")),
        check_vma=False,
    )
```

```python
import functools
import math

import jax
import jax.numpy as jnp
import numpy as np
from jax import lax
from jax.experimental import pallas as pl
from jax.experimental.pallas import tpu as pltpu
from jax.sharding import PartitionSpec as P

D = 3072
HD = 128
COLS = 128
HEADS = 7
MINE = 3
UNITS = 7
TOK = 128
FEAT = HEADS * HD
HALF = TOK // 2
PIECES = 6
STEP = D // PIECES
SCALE2 = math.log2(math.e) / math.sqrt(HD)
F32 = jnp.float32
HBM = "hbm"
BF16 = jnp.bfloat16
MIB = 1024 * 1024
COST = pl.CostEstimate(flops=1, transcendentals=0, bytes_accessed=1)
SMEM = pl.BlockSpec(memory_space=pltpu.SMEM)
VMEM = pl.BlockSpec(memory_space=pltpu.VMEM)
ANY = pl.BlockSpec(memory_space=pl.ANY)


def _place(x, y, z, c):
    return ((x * 2 + y) * 4 + z) * 2 + c


def _perm(move):
    pairs = []
    for p in range(64):
        x, y, z, c = p // 16, (p // 8) % 2, (p // 2) % 4, p % 2
        pairs.append((p, _place(*move(x, y, z, c))))
    return pairs


def _key_move(d):
    return lambda x, y, z, c: ((x + d) % 4, y, z, c) if c == 0 else (x, y, (z + d) % 4, c)


def _query_move(d):
    return lambda x, y, z, c: (x, y, (z + d) % 4, c) if c == 0 else ((x + d) % 4, y, z, c)


def _core_move(x, y, z, c):
    return (x, y, z, 1 - c)


def _y_move(x, y, z, c):
    return (x, 1 - y, z, c)


def move(array, how):
    return lax.ppermute(array, "patch", _perm(how))


def swap_heads(array):
    return lax.ppermute(array, "head", [(0, 1), (1, 0)])


def kernel_call(kernel, name, out_shape, scratch_shapes, place, scalars, *arrays, after=(), outside=(), limit=12):
    scalars = [*place, *scalars]
    begin, first, count = len(place), len(scalars) + len(outside) + len(arrays), len(after)

    def run(*refs):
        head = [[ref[0] for ref in refs[:begin]]] if begin else []
        kernel(*head, *refs[begin:first], *refs[first + count :])

    return pl.pallas_call(
        run,
        in_specs=[SMEM] * len(scalars) + [ANY] * len(outside) + [VMEM] * len(arrays) + [ANY] * count,
        out_specs=[VMEM] * len(out_shape),
        out_shape=[pltpu.VMEM(*s) if len(s) == 2 else jax.ShapeDtypeStruct(*s[:2]) for s in out_shape],
        scratch_shapes=[pltpu.VMEM(*s) if isinstance(s, tuple) else s for s in scratch_shapes],
        compiler_params=pltpu.CompilerParams(vmem_limit_bytes=limit * MIB),
        cost_estimate=COST,
        name=name,
    )(*scalars, *(pltpu.with_memory_space_constraint(a, pltpu.HBM) for a in outside), *arrays, *after)


def _turn(v, table_ref, which):
    v = v * lax.rsqrt(jnp.mean(v * v, axis=-1, keepdims=True) + 1e-06)
    lane = lax.broadcasted_iota(jnp.int32, v.shape, 1)
    other = jnp.where(lane % 2 == 0, pltpu.roll(v, HD - 1, 1), pltpu.roll(v, 1, 1))
    return v * table_ref[2 * which] + other * table_ref[2 * which + 1]


def _bring(w_ref, which, out_ref, sems):
    groups = []
    for j, i in enumerate(which):
        copies = []
        for k in range(PIECES):
            rows = pl.ds(k * STEP, STEP)
            copies.append(pltpu.make_async_copy(w_ref.at[i, rows], out_ref.at[j, rows], sems.at[j * PIECES + k]))
        for copy in copies:
            copy.start()
        groups.append(copies)
    return groups


def _stage_kernel(w_ref, image_ref, g_ref, turn_ref, out_ref, own_ref, table_ref, gain_ref, sems, more):
    copies = _bring(w_ref, (0,), out_ref, sems)[0]
    small = [pltpu.make_async_copy(g_ref, gain_ref, more.at[0]), pltpu.make_async_copy(image_ref, own_ref, more.at[1])]
    for copy in small:
        copy.start()
    small[0].wait()
    even = _lane((8, HD)) % 2 == 0
    for i in range(2):
        gain = jnp.broadcast_to(gain_ref[i : i + 1, :], (8, HD))
        swapped = jnp.where(even, pltpu.roll(gain, HD - 1, 1), pltpu.roll(gain, 1, 1))
        table_ref[2 * i] = turn_ref[0] * gain[0:1]
        table_ref[2 * i + 1] = turn_ref[1] * swapped[0:1]
    for copy in copies:
        copy.wait()
    small[1].wait()


def stage(w, image, gain, turns, after):
    scratch = [((2, HD), F32), pltpu.SemaphoreType.DMA((PIECES,)), pltpu.SemaphoreType.DMA((2,))]
    outs = [((1, D, FEAT), BF16), (image.shape, BF16), ((4, TOK, HD), F32)]
    return kernel_call(_stage_kernel, "stage", outs, scratch, [], [], turns, outside=[w, image, gain], after=after)


def _query_kernel(place, w_ref, oth_ref, own_ref, table_ref, qa_ref, qb_ref, q_ref, x_ref):
    x = jnp.concatenate([oth_ref[...], own_ref[...]], axis=0)
    x_ref[...] = x
    projected = jnp.dot(x, w_ref[0], preferred_element_type=F32)
    queries = []
    for head in range(HEADS):
        at = slice(head * HD, (head + 1) * HD)
        queries.append((_turn(projected[:, at], table_ref, 0) * SCALE2).astype(BF16))
        q_ref[head] = queries[head]
    qa_ref[MINE] = queries[MINE]
    first = place[0] == 0
    for i in range(MINE):
        low, high = queries[i], queries[i + MINE + 1]
        qa_ref[i] = jnp.where(first, low, high)
        qb_ref[i] = jnp.where(first, high, low)


def project_queries(place, *arrays):
    outs = [
        ((MINE + 1, TOK, HD), BF16),
        ((MINE, TOK, HD), BF16),
        ((HEADS, TOK, HD), BF16),
        ((TOK, D), BF16),
    ]
    return kernel_call(_query_kernel, "query_projection", outs, [], place, [], *arrays)


def _kv_kernel(place, w_ref, x_ref, table_ref, out_ref, kv_ref):
    first = pl.ds(pl.multiple_of((1 - place[1]) * HALF, HALF), HALF)
    second = pl.ds(pl.multiple_of(place[1] * HALF, HALF), HALF)
    projected = jnp.dot(x_ref[...], w_ref[1], preferred_element_type=F32)
    for head in range(HEADS):
        at = slice(head * HD, (head + 1) * HD)
        k = _turn(projected[:, at], table_ref, 1).astype(BF16)
        out_ref[0, first, at] = k[:HALF]
        out_ref[0, second, at] = k[HALF:]
        kv_ref[0, :, at] = k
    v = jnp.dot(x_ref[...], w_ref[2], preferred_element_type=F32).astype(BF16)
    out_ref[1, first, :] = v[:HALF]
    out_ref[1, second, :] = v[HALF:]
    kv_ref[1] = v


def project_keys(place, *arrays, after):
    outs = [((2, TOK, FEAT), BF16, HBM), ((2, TOK, FEAT), BF16)]
    return kernel_call(_kv_kernel, "key_value_projection", outs, [], place, [], *arrays, after=after)


def _home_kernel(count, text, q_ref, kv_ref, home_ref, stat_ref, s_ref):
    slots = text.shape[1]

    def score(head):
        at = slice(head * HD, (head + 1) * HD)
        s_ref[head, :, slots:] = _scores(q_ref[head], kv_ref[0, :, at])
        s = _scores(q_ref[head], text[0, :, at])
        s_ref[head, :, :slots] = jnp.where(_lane(s.shape) < count[0], s, -jnp.inf)

    stat = jnp.zeros((TOK, HD), F32)
    score(0)
    for head in range(HEADS):
        if head + 1 < HEADS:
            score(head + 1)
        at = slice(head * HD, (head + 1) * HD)
        peak, out = _fold(s_ref[head], None, jnp.concatenate([text[1, :, at], kv_ref[1, :, at]], axis=0))
        total = out[:, HD:]
        home_ref[head] = (out[:, :HD] / total).astype(BF16)
        stat = jnp.where(_lane(stat.shape) == head, peak + jnp.log2(total), stat)
    stat_ref[...] = stat


def attend_home(count, text_kv, *arrays, after):
    outs = [((HEADS, TOK, HD), BF16), ((TOK, HD), F32)]
    scratch = [((HEADS, TOK, text_kv.shape[1] + TOK), F32)]
    return kernel_call(_home_kernel, "home_attention", outs, scratch, [], [count], text_kv, *arrays, after=after)


def _join_kernel(a_ref, b_ref, out_ref):
    out_ref[: MINE + 1] = a_ref[...]
    out_ref[MINE + 1 :] = b_ref[...]


def _gate_kernel(a_ref, *refs):
    del a_ref, refs


def gate(array, after):
    return pl.pallas_call(
        _gate_kernel,
        in_specs=[ANY] * (1 + len(after)),
        out_specs=ANY,
        out_shape=pltpu.VMEM(array.shape, array.dtype),
        input_output_aliases={0: 0},
        compiler_params=pltpu.CompilerParams(vmem_limit_bytes=MIB),
        cost_estimate=COST,
        name="gate",
    )(pltpu.with_memory_space_constraint(array, pltpu.VMEM), *after)


def join_units(a, b, after):
    outs = [((UNITS, TOK, HD), BF16)]
    return kernel_call(_join_kernel, "join_units", outs, [], [], [], a, b, after=after)[0]


def _scores(q, k):
    return lax.dot_general(q, k, (((1,), (1,)), ((), ())), preferred_element_type=F32)


def _fold(s, peak, values):
    top = s[:, :HD]
    for t in range(1, s.shape[1] // HD):
        top = jnp.maximum(top, s[:, t * HD : (t + 1) * HD])
    top = jnp.max(top, axis=1, keepdims=True)
    if peak is not None:
        top = jnp.maximum(top, peak)
    raw = jnp.exp2(s - top).astype(BF16)
    wide = jnp.concatenate([values, jnp.ones((values.shape[0], HD), BF16)], axis=1)
    return top, jnp.dot(raw, wide, preferred_element_type=F32)


def _lane(shape):
    return lax.broadcasted_iota(jnp.int32, shape, 1)


def _put(stat, u, peak, total):
    lane = _lane(stat.shape)
    return jnp.where(lane == u, peak, jnp.where(lane == u + 16, total, stat))


def _cols(index):
    return pl.ds(pl.multiple_of(index * HD, HD), HD)


def _slot_of(u, c):
    if u == MINE:
        return MINE * (1 - c)
    return (u if u < MINE else u - MINE - 1) + c


ORDER = ((1, 2, 3, 0), (0, 1, 2, 3))
OWN = (slice(3 * HALF, 4 * HALF), slice(0, HALF))
ROWS = (((1, 0), (2, 0), (3, 0)), ((0, 0), (0, 1), (1, 1), (2, 1), (3, 1)))


def _gather(refs, u, rows):
    return jnp.concatenate([refs[i][u, g * HALF : (g + 1) * HALF] for i, g in rows], axis=0)


def _near_kernel(place, *refs):
    queries, keys = refs[:4], refs[4:8]
    acc_ref, stat_ref, s_ref = refs[8:]
    c = place[0]
    steps = [(u, g) for u in range(UNITS) for g in range(2)]

    def score(i):
        u, g = steps[i]
        q = _gather(queries, u, [(r, g) for r in ORDER[g]])
        for b, k in enumerate(keys):
            s = _scores(q, k[0, :, _cols(_slot_of(u, c))])
            s_ref[i % 2, :, b * 2 * TOK : (b + 1) * 2 * TOK] = s
        patch = slice(0, TOK) if u <= MINE else slice(TOK, 2 * TOK)
        s_ref[i % 2, OWN[g], patch] = jnp.full((HALF, TOK), -jnp.inf, F32)

    stats = [jnp.zeros((4 * HALF, HD), F32)] * 2
    score(0)
    for i, (u, g) in enumerate(steps):
        if i + 1 < len(steps):
            score(i + 1)
        values = jnp.concatenate([k[1, :, _cols(_slot_of(u, c))] for k in keys], axis=0)
        peak, out = _fold(s_ref[i % 2], None, values)
        acc_ref[u, g * 4 * HALF : (g + 1) * 4 * HALF] = out[:, :HD]
        stats[g] = _put(stats[g], u, peak, out[:, HD:])
    stat_ref[: 4 * HALF] = stats[0]
    stat_ref[4 * HALF :] = stats[1]


def attend_near(place, queries, pairs, after):
    outs = [((UNITS, 4 * TOK, HD), F32), ((4 * TOK, HD), F32)]
    scratch = [((2, 4 * HALF, 8 * TOK), F32)]
    return kernel_call(_near_kernel, "near_attention", outs, scratch, place, [], *queries, *pairs, after=after)


def _far_kernel(g, place, *refs):
    queries, (acc_in, stat_in), keys = refs[:4], refs[4:6], refs[6:10]
    outs, s_ref = refs[10:-1], refs[-1]
    c = place[0]
    count = len(ROWS[g]) * HALF
    rows = slice(0, count) if g == 0 else slice(4 * TOK - count, 4 * TOK)

    def score(u):
        q = _gather(queries, u, ROWS[g])
        for b, k in enumerate(keys):
            s = _scores(q, k[0, :, _cols(_slot_of(u, c))])
            s_ref[u % 2, :, b * 2 * TOK : (b + 1) * 2 * TOK] = s

    mark = jnp.zeros((count, HD), F32)
    score(0)
    for u in range(UNITS):
        if u + 1 < UNITS:
            score(u + 1)
        before = stat_in[rows, u : u + 1]
        values = jnp.concatenate([k[1, :, _cols(_slot_of(u, c))] for k in keys], axis=0)
        peak, out = _fold(s_ref[u % 2], before, values)
        factor = jnp.exp2(before - peak)
        total = stat_in[rows, u + 16 : u + 17] * factor + out[:, HD:]
        out = ((acc_in[u, rows] * factor + out[:, :HD]) / total).astype(BF16)
        level = peak + jnp.log2(total)
        mark = jnp.where(_lane(level.shape) % 16 == u, level, mark)
        _deal(outs, u, out)
    _deal(outs, UNITS, _spread(mark))


def _deal(outs, u, rows):
    at = 0
    for o in outs:
        o[u] = rows[at : at + o.shape[1]]
        at += o.shape[1]


def attend_far(g, place, queries, acc, stat, pairs, after):
    outs = [((UNITS + 1, HALF, HD), BF16)] * 3
    if g == 1:
        outs = [((UNITS + 1, TOK, HD), BF16)] + outs
    scratch = [((2, len(ROWS[g]) * HALF, 8 * TOK), F32)]
    kernel = functools.partial(_far_kernel, g)
    arrays = (*queries, acc, stat, *pairs)
    return kernel_call(kernel, f"far_attention_{g}", outs, scratch, place, [], *arrays, after=after)


def _spread(level):
    high = level.astype(BF16).astype(F32)
    middle = (level - high).astype(BF16).astype(F32)
    lane = _lane(level.shape)
    low = level - high - middle
    return jnp.where(lane < 16, high, jnp.where(lane < 32, middle, low)).astype(BF16)


def _collect(mark):
    mark = mark.astype(F32)
    return mark + pltpu.roll(mark, HD - 16, 1) + pltpu.roll(mark, HD - 32, 1)


def _merge_kernel(g, p0, p1, p2, p3, mine_ref, stat_ref, sib_ref):
    parts = (p0.at[:, g * HALF : (g + 1) * HALF], p1, p2, p3)
    levels = [_collect(p[UNITS]) for p in parts]
    top = functools.reduce(jnp.maximum, levels)
    weights = [jnp.exp2(v - top) for v in levels]
    total = functools.reduce(jnp.add, weights)
    weights = [w / total for w in weights]
    for u in range(UNITS):
        out = None
        for p, w in zip(parts, weights, strict=True):
            term = p[u].astype(F32) * w[:, u : u + 1]
            out = term if out is None else out + term
        if u <= MINE:
            mine_ref[u] = out.astype(BF16)
        else:
            sib_ref[u - MINE - 1] = out.astype(BF16)
    level = top + jnp.log2(total)
    stat_ref[...] = level
    lane = _lane(level.shape)
    level = jnp.where(lane < 16, level, 0.0)
    sib_ref[MINE] = _spread(level + pltpu.roll(level, 16, 1) + pltpu.roll(level, 32, 1))


def merge(g, parts):
    outs = [((MINE + 1, HALF, HD), BF16), ((HALF, HD), F32), ((MINE + 1, HALF, HD), BF16)]
    return kernel_call(functools.partial(_merge_kernel, g), "merge_parts", outs, [], [], [], *parts)


def _blend(a, la, h, lh):
    top = jnp.maximum(la, lh)
    wa, wh = jnp.exp2(la - top), jnp.exp2(lh - top)
    total = wa + wh
    return (a.astype(F32) * (wa / total) + h.astype(F32) * (wh / total)).astype(BF16)


def _rows(head):
    return pl.ds(pl.multiple_of(head * HD, HD), HD)


def _mine_kernel(g, place, mine_ref, stat_ref, home_ref, level_ref, w_ref, out_ref):
    rows = slice(g * HALF, (g + 1) * HALF)
    c = place[0]
    low, mine, level = c == 0, stat_ref[...], level_ref[rows]
    attended, weights = [], []
    for slot in range(MINE + 1):
        high = slot if slot == MINE else slot + MINE + 1
        head = slot + (high - slot) * c
        lh = jnp.where(low, level[:, slot : slot + 1], level[:, high : high + 1])
        attended.append(_blend(mine_ref[slot], mine[:, slot : slot + 1], home_ref[head, rows], lh))
        weights.append(w_ref[_rows(head), :])
    attended, weights = jnp.concatenate(attended, axis=1), jnp.concatenate(weights, axis=0)
    out_ref[...] = jnp.dot(attended, weights, preferred_element_type=F32)


def _got_kernel(g, place, part_ref, got_ref, home_ref, level_ref, w_ref, *rest):
    *other, out_ref = rest
    rows = slice(g * HALF, (g + 1) * HALF)
    c = place[0]
    low, level = c == 0, level_ref[rows]
    got = _collect(got_ref[MINE])
    attended, weights = [], []
    for slot in range(MINE):
        high = slot + MINE + 1
        head = high - (high - slot) * c
        lh = jnp.where(low, level[:, high : high + 1], level[:, slot : slot + 1])
        attended.append(_blend(got_ref[slot], got[:, high : high + 1], home_ref[head, rows], lh))
        weights.append(w_ref[_rows(head), :])
    attended, weights = jnp.concatenate(attended, axis=1), jnp.concatenate(weights, axis=0)
    out = part_ref[...] + jnp.dot(attended, weights, preferred_element_type=F32)
    for ref in other:
        out = out + ref[...].astype(F32)
    out_ref[...] = out.astype(BF16)


def project_out(g, place, mine, stat, got, home, level, w_out, *other):
    outs = [((HALF, D), F32)]
    arrays = (mine, stat, home, level, w_out)
    kernel = functools.partial(_mine_kernel, g)
    part = kernel_call(kernel, "output_projection_mine", outs, [], place, [], *arrays)[0]
    outs = [((HALF, D), BF16, HBM)]
    arrays = (part, got, home, level, w_out, *other)
    kernel = functools.partial(_got_kernel, g)
    return kernel_call(kernel, "output_projection_got", outs, [], place, [], *arrays)[0]


def _bands():
    first = HD // 8
    band = (HD - first) // 2
    omega = np.repeat(10000.0 ** (-2.0 * np.arange(band // 2) / band), 2)
    along_rows = np.zeros((HD,))
    along_cols = np.zeros((HD,))
    along_rows[first : first + band] = omega
    along_cols[first + band :] = omega
    sign = np.where(np.arange(HD) % 2 == 0, -1.0, 1.0)
    return (v.astype(np.float32) for v in (along_rows, along_cols, sign))


def body(image, w_qkv, qk_gain, stale_kv, text_kv, text_count, row_offset, w_out):
    core = lax.axis_index("patch") % 2
    group = lax.axis_index("head")
    place = [core.astype(jnp.int32).reshape(1), group.astype(jnp.int32).reshape(1)]
    other_image = swap_heads(image)

    wide = (2, TOK, (MINE + 1) * HD)
    given = lax.dynamic_slice(stale_kv, (0, 0, (1 - core) * MINE * HD), wide)
    kept = lax.dynamic_slice(stale_kv, (0, 0, core * MINE * HD), wide)
    pair = jnp.concatenate([kept, move(given, _core_move)], axis=1)
    far_pair = move(pair, _y_move)
    near = [pair] + [move(pair, _key_move(d)) for d in (1, 3, 2)]

    within = jnp.arange(TOK, dtype=jnp.int32)
    within = jnp.where(within < HALF, within + (1 - group) * HALF, within - (1 - group) * HALF)
    rows = (row_offset[0] + within // COLS).astype(F32)[:, None]
    cols = (within % COLS).astype(F32)[:, None]
    along_rows, along_cols, sign = _bands()
    angles = rows * along_rows + cols * along_cols
    turns = jnp.stack([jnp.cos(angles), jnp.sin(angles) * sign])

    w = jnp.transpose(w_qkv, (1, 0, 2))
    staged, own_image, table = stage(w, image, qk_gain, turns, [pair])
    q_mine, q_given, q_own, x = project_queries(place, staged, other_image, own_image, table)
    units = join_units(q_mine, move(q_given, _core_move), near[1:3])
    queries = [units] + [move(units, _query_move(d)) for d in (1, 3, 2)]
    far_two = move(near[3], _y_move)
    fresh_kv, kv = project_keys(place, w, x, table, after=[units, near[3]])
    far_pair = gate(far_pair, queries[1:4] + [kv])
    far = [far_pair] + [move(far_pair, _key_move(d)) for d in (1, 3)] + [far_two]
    home, level = attend_home(text_count, text_kv, q_own, kv, after=[far_pair])
    acc, stat = attend_near(place, queries, near, [home])

    first = attend_far(0, place, queries, acc, stat, far, [])
    own, *second = attend_far(1, place, queries, acc, stat, far, [])
    back = [[own] + [move(p, _query_move(d)) for p, d in zip(first, (3, 1, 2))]]
    back.append([own] + [move(second[i], _query_move(d)) for i, d in ((2, 2), (0, 3), (1, 1))])
    merged = [merge(g, back[g]) for g in (0, 1)]
    got = [move(merged[g][2], _core_move) for g in (0, 1)]
    sent = project_out(0, place, *merged[0][:2], got[0], home, level, w_out)
    mixed = project_out(1, place, *merged[1][:2], got[1], home, level, w_out, swap_heads(sent))
    return (mixed, fresh_kv)


def solution(mesh):
    placed = (
        P(("patch", "head"), None),
        P(None, None, "head"),
        P(),
        P(None, "patch", "head"),
        P(None, None, "head"),
        P(),
        P("patch"),
        P("head", None),
    )
    return jax.shard_map(
        body,
        mesh=mesh,
        in_specs=placed,
        out_specs=(P(("patch", "head"), None), P(None, "patch", "head")),
        check_vma=False,
    )
```

```python
import functools
import math

import jax
import jax.numpy as jnp
import numpy as np
from jax import lax
from jax.experimental import pallas as pl
from jax.experimental.pallas import tpu as pltpu
from jax.sharding import PartitionSpec as P

D = 3072
HD = 128
COLS = 128
HEADS = 7
MINE = 3
UNITS = 7
TOK = 128
FEAT = HEADS * HD
HALF = TOK // 2
PIECES = 6
STEP = D // PIECES
SCALE2 = math.log2(math.e) / math.sqrt(HD)
F32 = jnp.float32
HBM = "hbm"
BF16 = jnp.bfloat16
MIB = 1024 * 1024
COST = pl.CostEstimate(flops=1, transcendentals=0, bytes_accessed=1)
SMEM = pl.BlockSpec(memory_space=pltpu.SMEM)
VMEM = pl.BlockSpec(memory_space=pltpu.VMEM)
ANY = pl.BlockSpec(memory_space=pl.ANY)


def _place(x, y, z, c):
    return ((x * 2 + y) * 4 + z) * 2 + c


def _perm(move):
    pairs = []
    for p in range(64):
        x, y, z, c = p // 16, (p // 8) % 2, (p // 2) % 4, p % 2
        pairs.append((p, _place(*move(x, y, z, c))))
    return pairs


def _key_move(d):
    return lambda x, y, z, c: ((x + d) % 4, y, z, c) if c == 0 else (x, y, (z + d) % 4, c)


def _query_move(d):
    return lambda x, y, z, c: (x, y, (z + d) % 4, c) if c == 0 else ((x + d) % 4, y, z, c)


def _core_move(x, y, z, c):
    return (x, y, z, 1 - c)


def _y_move(x, y, z, c):
    return (x, 1 - y, z, c)


def move(array, how):
    return lax.ppermute(array, "patch", _perm(how))


def swap_heads(array):
    return lax.ppermute(array, "head", [(0, 1), (1, 0)])


def kernel_call(kernel, name, out_shape, scratch_shapes, place, scalars, *arrays, after=(), outside=(), limit=12):
    scalars = [*place, *scalars]
    begin, first, count = len(place), len(scalars) + len(outside) + len(arrays), len(after)

    def run(*refs):
        head = [[ref[0] for ref in refs[:begin]]] if begin else []
        kernel(*head, *refs[begin:first], *refs[first + count :])

    return pl.pallas_call(
        run,
        in_specs=[SMEM] * len(scalars) + [ANY] * len(outside) + [VMEM] * len(arrays) + [ANY] * count,
        out_specs=[VMEM] * len(out_shape),
        out_shape=[pltpu.VMEM(*s) if len(s) == 2 else jax.ShapeDtypeStruct(*s[:2]) for s in out_shape],
        scratch_shapes=[pltpu.VMEM(*s) if isinstance(s, tuple) else s for s in scratch_shapes],
        compiler_params=pltpu.CompilerParams(vmem_limit_bytes=limit * MIB),
        cost_estimate=COST,
        name=name,
    )(*scalars, *(pltpu.with_memory_space_constraint(a, pltpu.HBM) for a in outside), *arrays, *after)


def _turn(v, table_ref, which):
    v = v * lax.rsqrt(jnp.mean(v * v, axis=-1, keepdims=True) + 1e-06)
    lane = lax.broadcasted_iota(jnp.int32, v.shape, 1)
    other = jnp.where(lane % 2 == 0, pltpu.roll(v, HD - 1, 1), pltpu.roll(v, 1, 1))
    return v * table_ref[2 * which] + other * table_ref[2 * which + 1]


def _bring(w_ref, which, out_ref, sems):
    groups = []
    for j, i in enumerate(which):
        copies = []
        for k in range(PIECES):
            rows = pl.ds(k * STEP, STEP)
            copies.append(pltpu.make_async_copy(w_ref.at[i, rows], out_ref.at[j, rows], sems.at[j * PIECES + k]))
        for copy in copies:
            copy.start()
        groups.append(copies)
    return groups


def _stage_kernel(w_ref, image_ref, g_ref, turn_ref, out_ref, own_ref, table_ref, gain_ref, sems, more):
    copies = _bring(w_ref, (0,), out_ref, sems)[0]
    small = [pltpu.make_async_copy(g_ref, gain_ref, more.at[0]), pltpu.make_async_copy(image_ref, own_ref, more.at[1])]
    for copy in small:
        copy.start()
    small[0].wait()
    even = _lane((8, HD)) % 2 == 0
    for i in range(2):
        gain = jnp.broadcast_to(gain_ref[i : i + 1, :], (8, HD))
        swapped = jnp.where(even, pltpu.roll(gain, HD - 1, 1), pltpu.roll(gain, 1, 1))
        table_ref[2 * i] = turn_ref[0] * gain[0:1]
        table_ref[2 * i + 1] = turn_ref[1] * swapped[0:1]
    for copy in copies:
        copy.wait()
    small[1].wait()


def stage(w, image, gain, turns, after):
    scratch = [((2, HD), F32), pltpu.SemaphoreType.DMA((PIECES,)), pltpu.SemaphoreType.DMA((2,))]
    outs = [((1, D, FEAT), BF16), (image.shape, BF16), ((4, TOK, HD), F32)]
    return kernel_call(_stage_kernel, "stage", outs, scratch, [], [], turns, outside=[w, image, gain], after=after)


def _query_kernel(place, w_ref, oth_ref, own_ref, table_ref, qa_ref, qb_ref, q_ref, x_ref):
    x = jnp.concatenate([oth_ref[...], own_ref[...]], axis=0)
    x_ref[...] = x
    projected = jnp.dot(x, w_ref[0], preferred_element_type=F32)
    queries = []
    for head in range(HEADS):
        at = slice(head * HD, (head + 1) * HD)
        queries.append((_turn(projected[:, at], table_ref, 0) * SCALE2).astype(BF16))
        q_ref[head] = queries[head]
    qa_ref[MINE] = queries[MINE]
    first = place[0] == 0
    for i in range(MINE):
        low, high = queries[i], queries[i + MINE + 1]
        qa_ref[i] = jnp.where(first, low, high)
        qb_ref[i] = jnp.where(first, high, low)


def project_queries(place, *arrays):
    outs = [
        ((MINE + 1, TOK, HD), BF16),
        ((MINE, TOK, HD), BF16),
        ((HEADS, TOK, HD), BF16),
        ((TOK, D), BF16),
    ]
    return kernel_call(_query_kernel, "query_projection", outs, [], place, [], *arrays)


def _kv_kernel(place, w_ref, x_ref, table_ref, out_ref, kv_ref):
    first = pl.ds(pl.multiple_of((1 - place[1]) * HALF, HALF), HALF)
    second = pl.ds(pl.multiple_of(place[1] * HALF, HALF), HALF)
    projected = jnp.dot(x_ref[...], w_ref[1], preferred_element_type=F32)
    for head in range(HEADS):
        at = slice(head * HD, (head + 1) * HD)
        k = _turn(projected[:, at], table_ref, 1).astype(BF16)
        out_ref[0, first, at] = k[:HALF]
        out_ref[0, second, at] = k[HALF:]
        kv_ref[0, :, at] = k
    v = jnp.dot(x_ref[...], w_ref[2], preferred_element_type=F32).astype(BF16)
    out_ref[1, first, :] = v[:HALF]
    out_ref[1, second, :] = v[HALF:]
    kv_ref[1] = v


def project_keys(place, *arrays, after):
    outs = [((2, TOK, FEAT), BF16, HBM), ((2, TOK, FEAT), BF16)]
    return kernel_call(_kv_kernel, "key_value_projection", outs, [], place, [], *arrays, after=after)


def _home_kernel(count, text, q_ref, kv_ref, home_ref, stat_ref, s_ref):
    slots = text.shape[1]

    def score(head):
        at = slice(head * HD, (head + 1) * HD)
        s_ref[head, :, slots:] = _scores(q_ref[head], kv_ref[0, :, at])
        s = _scores(q_ref[head], text[0, :, at])
        s_ref[head, :, :slots] = jnp.where(_lane(s.shape) < count[0], s, -jnp.inf)

    stat = jnp.zeros((TOK, HD), F32)
    score(0)
    for head in range(HEADS):
        if head + 1 < HEADS:
            score(head + 1)
        at = slice(head * HD, (head + 1) * HD)
        peak, out = _fold(s_ref[head], None, jnp.concatenate([text[1, :, at], kv_ref[1, :, at]], axis=0))
        total = out[:, HD:]
        home_ref[head] = (out[:, :HD] / total).astype(BF16)
        stat = jnp.where(_lane(stat.shape) == head, peak + jnp.log2(total), stat)
    stat_ref[...] = stat


def attend_home(count, text_kv, *arrays, after):
    outs = [((HEADS, TOK, HD), BF16), ((TOK, HD), F32)]
    scratch = [((HEADS, TOK, text_kv.shape[1] + TOK), F32)]
    return kernel_call(_home_kernel, "home_attention", outs, scratch, [], [count], text_kv, *arrays, after=after)


def _join_kernel(a_ref, b_ref, out_ref):
    out_ref[: MINE + 1] = a_ref[...]
    out_ref[MINE + 1 :] = b_ref[...]


def _gate_kernel(a_ref, *refs):
    del a_ref, refs


def gate(array, after):
    return pl.pallas_call(
        _gate_kernel,
        in_specs=[ANY] * (1 + len(after)),
        out_specs=ANY,
        out_shape=pltpu.VMEM(array.shape, array.dtype),
        input_output_aliases={0: 0},
        compiler_params=pltpu.CompilerParams(vmem_limit_bytes=MIB),
        cost_estimate=COST,
        name="gate",
    )(pltpu.with_memory_space_constraint(array, pltpu.VMEM), *after)


def join_units(a, b, after):
    outs = [((UNITS, TOK, HD), BF16)]
    return kernel_call(_join_kernel, "join_units", outs, [], [], [], a, b, after=after)[0]


def _scores(q, k):
    return lax.dot_general(q, k, (((1,), (1,)), ((), ())), preferred_element_type=F32)


def _fold(s, peak, values):
    top = s[:, :HD]
    for t in range(1, s.shape[1] // HD):
        top = jnp.maximum(top, s[:, t * HD : (t + 1) * HD])
    top = jnp.max(top, axis=1, keepdims=True)
    if peak is not None:
        top = jnp.maximum(top, peak)
    raw = jnp.exp2(s - top).astype(BF16)
    wide = jnp.concatenate([values, jnp.ones((values.shape[0], HD), BF16)], axis=1)
    return top, jnp.dot(raw, wide, preferred_element_type=F32)


def _lane(shape):
    return lax.broadcasted_iota(jnp.int32, shape, 1)


def _put(stat, u, peak, total):
    lane = _lane(stat.shape)
    return jnp.where(lane == u, peak, jnp.where(lane == u + 16, total, stat))


def _cols(index):
    return pl.ds(pl.multiple_of(index * HD, HD), HD)


def _slot_of(u, c):
    if u == MINE:
        return MINE * (1 - c)
    return (u if u < MINE else u - MINE - 1) + c


ORDER = ((1, 2, 3, 0), (0, 1, 2, 3))
OWN = (slice(3 * HALF, 4 * HALF), slice(0, HALF))
ROWS = (((1, 0), (2, 0), (3, 0)), ((0, 0), (0, 1), (1, 1), (2, 1), (3, 1)))


def _gather(refs, u, rows):
    return jnp.concatenate([refs[i][u, g * HALF : (g + 1) * HALF] for i, g in rows], axis=0)


def _near_kernel(place, *refs):
    queries, keys = refs[:4], refs[4:8]
    acc_ref, stat_ref, s_ref = refs[8:]
    c = place[0]
    steps = [(u, g) for u in range(UNITS) for g in range(2)]

    def score(i):
        u, g = steps[i]
        q = _gather(queries, u, [(r, g) for r in ORDER[g]])
        for b, k in enumerate(keys):
            s = _scores(q, k[0, :, _cols(_slot_of(u, c))])
            s_ref[i % 2, :, b * 2 * TOK : (b + 1) * 2 * TOK] = s
        patch = slice(0, TOK) if u <= MINE else slice(TOK, 2 * TOK)
        s_ref[i % 2, OWN[g], patch] = jnp.full((HALF, TOK), -jnp.inf, F32)

    stats = [jnp.zeros((4 * HALF, HD), F32)] * 2
    score(0)
    for i, (u, g) in enumerate(steps):
        if i + 1 < len(steps):
            score(i + 1)
        values = jnp.concatenate([k[1, :, _cols(_slot_of(u, c))] for k in keys], axis=0)
        peak, out = _fold(s_ref[i % 2], None, values)
        acc_ref[u, g * 4 * HALF : (g + 1) * 4 * HALF] = out[:, :HD]
        stats[g] = _put(stats[g], u, peak, out[:, HD:])
    stat_ref[: 4 * HALF] = stats[0]
    stat_ref[4 * HALF :] = stats[1]


def attend_near(place, queries, pairs, after):
    outs = [((UNITS, 4 * TOK, HD), F32), ((4 * TOK, HD), F32)]
    scratch = [((2, 4 * HALF, 8 * TOK), F32)]
    return kernel_call(_near_kernel, "near_attention", outs, scratch, place, [], *queries, *pairs, after=after)


def _far_kernel(g, place, *refs):
    queries, (acc_in, stat_in), keys = refs[:4], refs[4:6], refs[6:10]
    outs, s_ref = refs[10:-1], refs[-1]
    c = place[0]
    count = len(ROWS[g]) * HALF
    rows = slice(0, count) if g == 0 else slice(4 * TOK - count, 4 * TOK)

    def score(u):
        q = _gather(queries, u, ROWS[g])
        for b, k in enumerate(keys):
            s = _scores(q, k[0, :, _cols(_slot_of(u, c))])
            s_ref[u % 2, :, b * 2 * TOK : (b + 1) * 2 * TOK] = s

    mark = jnp.zeros((count, HD), F32)
    score(0)
    for u in range(UNITS):
        if u + 1 < UNITS:
            score(u + 1)
        before = stat_in[rows, u : u + 1]
        values = jnp.concatenate([k[1, :, _cols(_slot_of(u, c))] for k in keys], axis=0)
        peak, out = _fold(s_ref[u % 2], before, values)
        factor = jnp.exp2(before - peak)
        total = stat_in[rows, u + 16 : u + 17] * factor + out[:, HD:]
        out = ((acc_in[u, rows] * factor + out[:, :HD]) / total).astype(BF16)
        level = peak + jnp.log2(total)
        mark = jnp.where(_lane(level.shape) % 16 == u, level, mark)
        _deal(outs, u, out)
    _deal(outs, UNITS, _spread(mark))


def _deal(outs, u, rows):
    at = 0
    for o in outs:
        o[u] = rows[at : at + o.shape[1]]
        at += o.shape[1]


def attend_far(g, place, queries, acc, stat, pairs, after):
    outs = [((UNITS + 1, HALF, HD), BF16)] * 3
    if g == 1:
        outs = [((UNITS + 1, TOK, HD), BF16)] + outs
    scratch = [((2, len(ROWS[g]) * HALF, 8 * TOK), F32)]
    kernel = functools.partial(_far_kernel, g)
    arrays = (*queries, acc, stat, *pairs)
    return kernel_call(kernel, f"far_attention_{g}", outs, scratch, place, [], *arrays, after=after)


def _spread(level):
    high = level.astype(BF16).astype(F32)
    middle = (level - high).astype(BF16).astype(F32)
    lane = _lane(level.shape)
    low = level - high - middle
    return jnp.where(lane < 16, high, jnp.where(lane < 32, middle, low)).astype(BF16)


def _collect(mark):
    mark = mark.astype(F32)
    return mark + pltpu.roll(mark, HD - 16, 1) + pltpu.roll(mark, HD - 32, 1)


def _merge_kernel(g, p0, p1, p2, p3, mine_ref, stat_ref, sib_ref):
    parts = (p0.at[:, g * HALF : (g + 1) * HALF], p1, p2, p3)
    levels = [_collect(p[UNITS]) for p in parts]
    top = functools.reduce(jnp.maximum, levels)
    weights = [jnp.exp2(v - top) for v in levels]
    total = functools.reduce(jnp.add, weights)
    weights = [w / total for w in weights]
    for u in range(UNITS):
        out = None
        for p, w in zip(parts, weights, strict=True):
            term = p[u].astype(F32) * w[:, u : u + 1]
            out = term if out is None else out + term
        if u <= MINE:
            mine_ref[u] = out.astype(BF16)
        else:
            sib_ref[u - MINE - 1] = out.astype(BF16)
    level = top + jnp.log2(total)
    stat_ref[...] = level
    lane = _lane(level.shape)
    level = jnp.where(lane < 16, level, 0.0)
    sib_ref[MINE] = _spread(level + pltpu.roll(level, 16, 1) + pltpu.roll(level, 32, 1))


def merge(g, parts):
    outs = [((MINE + 1, HALF, HD), BF16), ((HALF, HD), F32), ((MINE + 1, HALF, HD), BF16)]
    return kernel_call(functools.partial(_merge_kernel, g), "merge_parts", outs, [], [], [], *parts)


def _blend(a, la, h, lh):
    top = jnp.maximum(la, lh)
    wa, wh = jnp.exp2(la - top), jnp.exp2(lh - top)
    total = wa + wh
    return (a.astype(F32) * (wa / total) + h.astype(F32) * (wh / total)).astype(BF16)


def _rows(head):
    return pl.ds(pl.multiple_of(head * HD, HD), HD)


def _mine_kernel(g, place, mine_ref, stat_ref, home_ref, level_ref, w_ref, out_ref):
    rows = slice(g * HALF, (g + 1) * HALF)
    c = place[0]
    low, mine, level = c == 0, stat_ref[...], level_ref[rows]
    attended, weights = [], []
    for slot in range(MINE + 1):
        high = slot if slot == MINE else slot + MINE + 1
        head = slot + (high - slot) * c
        lh = jnp.where(low, level[:, slot : slot + 1], level[:, high : high + 1])
        attended.append(_blend(mine_ref[slot], mine[:, slot : slot + 1], home_ref[head, rows], lh))
        weights.append(w_ref[_rows(head), :])
    attended, weights = jnp.concatenate(attended, axis=1), jnp.concatenate(weights, axis=0)
    out_ref[...] = jnp.dot(attended, weights, preferred_element_type=F32)


def _got_kernel(g, place, part_ref, got_ref, home_ref, level_ref, w_ref, *rest):
    *other, out_ref = rest
    rows = slice(g * HALF, (g + 1) * HALF)
    c = place[0]
    low, level = c == 0, level_ref[rows]
    got = _collect(got_ref[MINE])
    attended, weights = [], []
    for slot in range(MINE):
        high = slot + MINE + 1
        head = high - (high - slot) * c
        lh = jnp.where(low, level[:, high : high + 1], level[:, slot : slot + 1])
        attended.append(_blend(got_ref[slot], got[:, high : high + 1], home_ref[head, rows], lh))
        weights.append(w_ref[_rows(head), :])
    attended, weights = jnp.concatenate(attended, axis=1), jnp.concatenate(weights, axis=0)
    out = part_ref[...] + jnp.dot(attended, weights, preferred_element_type=F32)
    for ref in other:
        out = out + ref[...].astype(F32)
    out_ref[...] = out.astype(BF16)


def project_out(g, place, mine, stat, got, home, level, w_out, *other):
    outs = [((HALF, D), F32)]
    arrays = (mine, stat, home, level, w_out)
    kernel = functools.partial(_mine_kernel, g)
    part = kernel_call(kernel, "output_projection_mine", outs, [], place, [], *arrays)[0]
    outs = [((HALF, D), BF16, HBM) if g == 1 else ((HALF, D), BF16)]
    arrays = (part, got, home, level, w_out, *other)
    kernel = functools.partial(_got_kernel, g)
    return kernel_call(kernel, "output_projection_got", outs, [], place, [], *arrays)[0]


def _bands():
    first = HD // 8
    band = (HD - first) // 2
    omega = np.repeat(10000.0 ** (-2.0 * np.arange(band // 2) / band), 2)
    along_rows = np.zeros((HD,))
    along_cols = np.zeros((HD,))
    along_rows[first : first + band] = omega
    along_cols[first + band :] = omega
    sign = np.where(np.arange(HD) % 2 == 0, -1.0, 1.0)
    return (v.astype(np.float32) for v in (along_rows, along_cols, sign))


def body(image, w_qkv, qk_gain, stale_kv, text_kv, text_count, row_offset, w_out):
    core = lax.axis_index("patch") % 2
    group = lax.axis_index("head")
    place = [core.astype(jnp.int32).reshape(1), group.astype(jnp.int32).reshape(1)]
    other_image = swap_heads(image)

    wide = (2, TOK, (MINE + 1) * HD)
    given = lax.dynamic_slice(stale_kv, (0, 0, (1 - core) * MINE * HD), wide)
    kept = lax.dynamic_slice(stale_kv, (0, 0, core * MINE * HD), wide)
    pair = jnp.concatenate([kept, move(given, _core_move)], axis=1)
    far_pair = move(pair, _y_move)
    near = [pair] + [move(pair, _key_move(d)) for d in (1, 3, 2)]

    within = jnp.arange(TOK, dtype=jnp.int32)
    within = jnp.where(within < HALF, within + (1 - group) * HALF, within - (1 - group) * HALF)
    rows = (row_offset[0] + within // COLS).astype(F32)[:, None]
    cols = (within % COLS).astype(F32)[:, None]
    along_rows, along_cols, sign = _bands()
    angles = rows * along_rows + cols * along_cols
    turns = jnp.stack([jnp.cos(angles), jnp.sin(angles) * sign])

    w = jnp.transpose(w_qkv, (1, 0, 2))
    staged, own_image, table = stage(w, image, qk_gain, turns, [pair])
    q_mine, q_given, q_own, x = project_queries(place, staged, other_image, own_image, table)
    units = join_units(q_mine, move(q_given, _core_move), near[1:3])
    queries = [units] + [move(units, _query_move(d)) for d in (1, 3, 2)]
    far_two = move(near[3], _y_move)
    fresh_kv, kv = project_keys(place, w, x, table, after=[units, near[3]])
    far_pair = gate(far_pair, queries[1:4] + [kv])
    far = [far_pair] + [move(far_pair, _key_move(d)) for d in (1, 3)] + [far_two]
    home, level = attend_home(text_count, text_kv, q_own, kv, after=[far_pair])
    acc, stat = attend_near(place, queries, near, [home])

    first = attend_far(0, place, queries, acc, stat, far, [])
    own, *second = attend_far(1, place, queries, acc, stat, far, [])
    back = [[own] + [move(p, _query_move(d)) for p, d in zip(first, (3, 1, 2))]]
    back.append([own] + [move(second[i], _query_move(d)) for i, d in ((2, 2), (0, 3), (1, 1))])
    merged = [merge(g, back[g]) for g in (0, 1)]
    got = [move(merged[g][2], _core_move) for g in (0, 1)]
    sent = project_out(0, place, *merged[0][:2], got[0], home, level, w_out)
    mixed = project_out(1, place, *merged[1][:2], got[1], home, level, w_out, swap_heads(sent))
    return (mixed, fresh_kv)


def solution(mesh):
    placed = (
        P(("patch", "head"), None),
        P(None, None, "head"),
        P(),
        P(None, "patch", "head"),
        P(None, None, "head"),
        P(),
        P("patch"),
        P("head", None),
    )
    return jax.shard_map(
        body,
        mesh=mesh,
        in_specs=placed,
        out_specs=(P(("patch", "head"), None), P(None, "patch", "head")),
        check_vma=False,
    )
```
